128 devices in a mesh: row: 16 (over y_hi, x, core), col: 8 (over z, y_lo).
Axes of the slice: x: 4, y: 4 (y_hi: 2, y_lo: 2; y = y_hi * 2 + y_lo), z: 4, core: 2. Of those that a mesh axis runs over, the one named last changes fastest.
Arguments:
- hidden: bfloat16 [2, 4096, 8192], P(None, 'row'), may hold values from -24 to 24
- wqkv: bfloat16 [8192, 10240], P('row', 'col'), may hold values from -0.09375 to 0.09375
- wo: bfloat16 [8192, 8192], P('row', 'col'), may hold values from -0.1875 to 0.1875
- picks: int32 [2, 32, 8], replicated, may hold values from 0 to 31, as said below
Outputs:
- mixed: bfloat16 [2, 4096, 8192], P(None, 'row', 'col')
The draws below stay inside these ranges and needn't reach their ends.
Inputs may be any that keep to these rules, and one draw needn't show every extreme that they name: `picks`: each row names 8 distinct blocks: the query block and the blocks before and after it (cyclically), then both end blocks unless already named, the rest at random.
All inputs are finite; a program needn't handle non-finite values.
Results may differ from the reference program's by a relative error of at most 0.012.
The reference program's roundings to bfloat16 on the way (of `query`, `weights` and `attn`) count: a program that leaves them out, or rounds other values in their place, can miss the bound.
Values may be sent and summed in bfloat16 or wider, within the bound.
No kernel may reach another device: no remote copies, remote signals or barrier semaphores. Data moves between devices by JAX's collectives and lax.ppermute only.
A program may use at most 192 MiB of HBM per device.

```python
import math
import jax
import jax.numpy as jnp
from jax import lax

D = 8192
HD = 128
KVH = 8
QH = 64
BLOCK = 128
KB = 8
SEQS = 2
G = 8
QKVC = 10240
LEN = 4096
NB = 32


def draw_hidden(key, part):
    first = jax.random.fold_in(key, 0)
    base = jax.random.normal(first, (SEQS, LEN, D), jnp.float32)
    base = jnp.clip(base, -6.0, 6.0)
    return jnp.clip(base, -24.0, 24.0).astype(jnp.bfloat16)


def draw_picks(key, part):
    inner = jax.random.fold_in(key, 17)
    block = jnp.arange(NB).astype(jnp.int32)
    window = (block[:, None] + jnp.arange(-1, 2).astype(jnp.int32)[None, :] + NB) % NB
    candidate = jnp.arange(NB).astype(jnp.int32)
    in_window = jnp.any(candidate[None, :, None] == window[:, None, :], axis=-1)
    noise = jax.random.randint(inner, (SEQS, NB, NB), 0, 1048576)
    score = noise * NB + candidate[None, None, :]
    ends = (candidate == 0) | (candidate == NB - 1)
    score = score + jnp.where(ends, 67108864, 0)[None, None, :]
    score = jnp.where(in_window[None, :, :], -1073741824, score)
    chosen = lax.top_k(score, KB - 3)[1].astype(jnp.int32)
    window_all = jnp.broadcast_to(window[None, :, :], (SEQS, NB, 3))
    return jnp.concatenate([window_all, chosen], axis=-1).astype(jnp.int32)


def block_scale(stream_key, shape, cuts, low, largest):
    factor_of, own = 1.0, jax.random.fold_in(stream_key, 6)
    for dim, blocks in cuts:
        heights = jnp.exp(jax.random.uniform(jax.random.fold_in(own, dim), (blocks,), jnp.float32, low / len(cuts), largest / len(cuts)))
        factor_of = factor_of * jnp.repeat(heights, shape[dim] // blocks).reshape([-1 if axis == dim else 1 for axis in range(len(shape))])
    return factor_of


def normal_values(rng, shape, width, bound, cuts=(), kind=jnp.bfloat16):
    entries = jax.random.normal(rng, shape, jnp.float32) * width
    if len(cuts) > 0:
        entries = block_scale(rng, shape, cuts, -0.22, 0.18) * entries
    return jnp.clip(entries, min=-bound, max=bound).astype(kind)


def setup_inputs(seed: int = 0) -> dict:
    arg_keys = jax.random.split(jax.random.key(seed), 5)
    return {
        "hidden": draw_hidden(jax.random.fold_in(arg_keys[4], 71), 0),
        "wqkv": normal_values(arg_keys[1], (D, QKVC), (D // 2) ** -0.5, 0.09375, ((0, 16), (1, 8))),
        "wo": normal_values(arg_keys[2], (QH * HD, D), (QH * HD // 8) ** -0.5, 0.1875, ((0, 16), (1, 8))),
        "picks": draw_picks(jax.random.fold_in(arg_keys[4], 71), 0),
    }


rope_base = 500000.0

def rope(tensor, positions):
    half = tensor.shape[-1] // 2
    index = jnp.arange(half).astype(jnp.float32)
    inverse = jnp.exp(-math.log(rope_base) * 2.0 * index / tensor.shape[-1])
    angle = positions.astype(jnp.float32)[:, None] * inverse[None, :]
    shape = (angle.shape[0],) + (1,) * (tensor.ndim - 3) + (half,)
    cosine = jnp.cos(angle).reshape(shape)
    sine = jnp.sin(angle).reshape(shape)
    first = tensor[..., :half]
    second = tensor[..., half:]
    return jnp.concatenate([first * cosine - second * sine, second * cosine + first * sine], axis=-1)

def attend(query_blocks, key_all, value_all, chosen):
    count = query_blocks.shape[0]
    key_sel = key_all[chosen].astype(jnp.float32)
    value_sel = value_all[chosen].astype(jnp.float32)
    scores = jnp.einsum('nqd,nkjd->nqkj', query_blocks.astype(jnp.float32), key_sel) * (1.0 / math.sqrt(HD))
    scores = scores.reshape(count, BLOCK, KB * BLOCK)
    top = lax.optimization_barrier(jnp.max(scores, axis=-1, keepdims=True))
    expo = jnp.exp(scores - top)
    weights = (expo / lax.optimization_barrier(jnp.sum(expo, axis=-1, keepdims=True))).astype(jnp.bfloat16)
    result = jnp.einsum('nqx,nxd->nqd', weights.astype(jnp.float32), value_sel.reshape(count, KB * BLOCK, HD))
    return result.astype(jnp.bfloat16)

def reference(hidden, wqkv, wo, picks):
    flat = hidden.reshape(SEQS * LEN, D)
    qkv = jnp.dot(flat, wqkv, preferred_element_type=jnp.float32).reshape(SEQS, LEN, KVH, G + 2, HD)
    positions = jnp.arange(LEN).astype(jnp.int32)
    query = rope(qkv[:, :, :, :G, :].reshape(SEQS, LEN, QH, HD), positions).astype(jnp.bfloat16)
    keys = rope(qkv[:, :, :, G, :], positions).astype(jnp.bfloat16)
    values = qkv[:, :, :, G + 1, :].astype(jnp.bfloat16)

    def per_seq(items):
        q_seq, k_seq, v_seq, chosen = items
        q_heads = q_seq.reshape(NB, BLOCK, QH, HD).transpose(2, 0, 1, 3)
        k_heads = k_seq.reshape(NB, BLOCK, KVH, HD).transpose(2, 0, 1, 3)
        v_heads = v_seq.reshape(NB, BLOCK, KVH, HD).transpose(2, 0, 1, 3)
        k_heads = jnp.repeat(k_heads, G, axis=0)
        v_heads = jnp.repeat(v_heads, G, axis=0)
        out = jax.vmap(attend, in_axes=(0, 0, 0, None))(q_heads, k_heads, v_heads, chosen)
        return out.transpose(1, 2, 0, 3).reshape(LEN, QH * HD)
    attn = lax.map(per_seq, (query, keys, values, picks))
    mixed = jnp.dot(attn.reshape(SEQS * LEN, QH * HD), wo, preferred_element_type=jnp.float32)
    return mixed.astype(jnp.bfloat16).reshape(SEQS, LEN, D)
```

```python
import functools
import math

import jax
import jax.numpy as jnp
from jax import lax
from jax.experimental import pallas as pl
from jax.experimental.pallas import tpu as pltpu
from jax.sharding import Mesh
from jax.sharding import PartitionSpec as P

HD = 128
BLOCK = 128
KB = 8
G = 8
rope_base = 500000.0
F32 = jnp.float32
BF16 = jnp.bfloat16


def shift(a, axis, step):
    n = 4
    return lax.ppermute(a, axis, [(i, (i + step) % n) for i in range(n)])


def swap(a, axis):
    return lax.ppermute(a, axis, [(0, 1), (1, 0)])


def ring(piece, axis):
    half = piece.shape[0] // 2
    left = shift(piece, axis, 1)
    right = shift(piece, axis, -1)
    far0 = shift(left[:half], axis, 1)
    far1 = shift(right[half:], axis, -1)
    return [[piece], [right], [far0, far1], [left]]


def spread(piece, pair_axis, ring_axis):
    other = swap(piece, pair_axis)
    return [ring(piece, ring_axis), ring(other, ring_axis)]


def tables(rows):
    half = HD // 2
    index = jnp.arange(half).astype(F32)
    inverse = jnp.exp(-math.log(rope_base) * 2.0 * index / HD)
    first = ((lax.axis_index("yh") * 4 + lax.axis_index("x")) * 2 + lax.axis_index("core")) * rows
    positions = first + jnp.arange(rows)
    angle = positions.astype(F32)[:, None] * inverse[None, :]
    cosine, sine = jnp.cos(angle), jnp.sin(angle)
    return jnp.concatenate([cosine, cosine], -1), jnp.concatenate([-sine, sine], -1)


def attend_kernel(idx, q_ref, cos_ref, sin_ref, kv_ref, out_ref):
    n = pl.program_id(0)
    cosine, sine = cos_ref[...], sin_ref[...]
    heads = []
    for g in range(G):
        t = q_ref[:, g * HD : (g + 1) * HD]
        heads.append((t * cosine + pltpu.roll(t, HD // 2, 1) * sine).astype(BF16))
    q = jnp.concatenate(heads, 0)
    keys = jnp.concatenate([kv_ref[idx[n, j], :, :HD] for j in range(KB)], 0)
    values = jnp.concatenate([kv_ref[idx[n, j], :, HD:] for j in range(KB)], 0)
    s = lax.dot_general(q, keys, (((1,), (1,)), ((), ())), preferred_element_type=F32)
    top = jnp.max(s, -1, keepdims=True)
    e = jnp.exp2((s - top) * (math.log2(math.e) / math.sqrt(HD)))
    total = jnp.sum(e, -1, keepdims=True)
    o = jnp.dot(e.astype(BF16), values, preferred_element_type=F32) / total
    o = o.astype(BF16)
    for g in range(G):
        out_ref[:, g * HD : (g + 1) * HD] = o[g * BLOCK : (g + 1) * BLOCK]


def attend(q, cosine, sine, kv, idx, lblocks):
    tiles = idx.shape[0]
    return pl.pallas_call(
        attend_kernel,
        grid_spec=pltpu.PrefetchScalarGridSpec(
            num_scalar_prefetch=1,
            grid=(tiles,),
            in_specs=[
                pl.BlockSpec((BLOCK, G * HD), lambda n, idx: (n, 0)),
                pl.BlockSpec((BLOCK, HD), lambda n, idx: (lax.rem(n, lblocks), 0)),
                pl.BlockSpec((BLOCK, HD), lambda n, idx: (lax.rem(n, lblocks), 0)),
                pl.BlockSpec(kv.shape, lambda n, idx: (0, 0, 0)),
            ],
            out_specs=pl.BlockSpec((BLOCK, G * HD), lambda n, idx: (n, 0)),
        ),
        out_shape=jax.ShapeDtypeStruct((tiles * BLOCK, G * HD), BF16),
        compiler_params=pltpu.CompilerParams(vmem_limit_bytes=48 * 2**20),
        cost_estimate=pl.CostEstimate(flops=2 * 10**9, bytes_accessed=8 * 10**6, transcendentals=4 * 10**6),
    )(idx, q, cosine, sine, kv)


def project(hidden, gathered, others):
    yh, x, core = lax.axis_index("yh"), lax.axis_index("x"), lax.axis_index("core")
    total = None
    for a in range(2):
        for b in range(4):
            for c, side in ((0, gathered), (1, others)):
                start = (((yh ^ a) * 4 + (x + b) % 4) * 2 + (core ^ c)) * 512
                for part in side[a][b]:
                    depth = part.shape[0]
                    cols = lax.dynamic_slice_in_dim(hidden, start, depth, 1)
                    term = jnp.dot(cols, part, preferred_element_type=F32)
                    total = term if total is None else total + term
                    start = start + depth
    return total


def cores(gathered):
    return jax.tree.map(lambda t: swap(t, "core"), gathered)


def on_device(hidden, wqkv, wo, picks):
    seqs, rows, feats = hidden.shape
    hidden = hidden.reshape(seqs * rows, feats)
    yh, x, core = lax.axis_index("yh"), lax.axis_index("x"), lax.axis_index("core")
    z, yl = lax.axis_index("z"), lax.axis_index("yl")
    lblocks = rows // BLOCK
    cosine, sine = tables(rows)

    w_kv, w_q = wqkv[:, G * HD :], wqkv[:, : G * HD]
    g_kv = spread(w_kv, "yh", "x")
    g_q = spread(w_q, "yh", "x")
    kv = project(hidden, g_kv, cores(g_kv))
    keys = kv[:, :HD].reshape(seqs, rows, HD)
    keys = keys * cosine + jnp.roll(keys, HD // 2, -1) * sine
    pair = jnp.concatenate([keys.reshape(seqs * rows, HD), kv[:, HD:]], -1).astype(BF16)
    g_pair = spread(pair, "yh", "x")
    sides = [g_pair, cores(g_pair)]
    flat = [part for side in sides for line in side for parts in line for part in parts]
    kv_all = jnp.concatenate(flat, 0).reshape(-1, BLOCK, 2 * HD)

    first = (yh * 4 + x) * 2 + core
    mine = lax.dynamic_slice_in_dim(picks, first * lblocks, lblocks, 1)
    owner, sub = mine // lblocks, mine % lblocks
    far = (owner // 2) % 4
    rel = ((owner % 2) ^ core) * 8 + ((owner // 8) ^ yh) * 4 + (far - x) % 4
    seq = jnp.arange(seqs)[:, None, None]
    idx = (rel * (seqs * lblocks) + seq * lblocks + sub).reshape(seqs * lblocks, KB)

    q = project(hidden, g_q, cores(g_q))
    attn = attend(q, cosine, sine, kv_all, idx.astype(jnp.int32), lblocks)

    g_wo = spread(wo, "yh", "x")
    o_wo = cores(g_wo)
    line = []
    for a in range(2):
        for b in range(4):
            line.append((jnp.concatenate(g_wo[a][b], 0), jnp.concatenate(o_wo[a][b], 0)))
    low = jnp.where(core == 0, 1, 0)
    buf = jnp.stack([jnp.where(core == 0, jnp.stack([m, o]), jnp.stack([o, m])) for m, o in line])
    buf = buf.reshape(8, 1024, wo.shape[1])

    g_attn = spread(attn, "yl", "z")
    total = None
    for a in range(2):
        for b in range(4):
            c = ((z + b) % 4) * 2 + (yl ^ a)
            place = ((c // 4) ^ yh) * 4 + (c % 4 - x) % 4
            w = lax.dynamic_index_in_dim(buf, place, 0, keepdims=False)
            start = 0
            half = attn.shape[0] // 2
            parts = g_attn[a][b]
            piece = parts[0] if len(parts) == 1 else jnp.concatenate(parts, 0)
            term = jnp.dot(piece, w, preferred_element_type=F32)
            total = term if total is None else total + term
    return total.astype(BF16).reshape(seqs, rows, -1)


def solution(mesh):
    fine = Mesh(mesh.devices.reshape(2, 4, 2, 4, 2), ("yh", "x", "core", "z", "yl"))
    row, col = ("yh", "x", "core"), ("z", "yl")
    return jax.shard_map(
        on_device,
        mesh=fine,
        in_specs=(P(None, row, None), P(row, col), P(row, col), P()),
        out_specs=P(None, row, col),
        check_vma=False,
    )
```

```python
import functools
import math

import jax
import jax.numpy as jnp
from jax import lax
from jax.experimental import pallas as pl
from jax.experimental.pallas import tpu as pltpu
from jax.sharding import Mesh
from jax.sharding import PartitionSpec as P

HD = 128
BLOCK = 128
KB = 8
G = 8
HALF = G // 2
rope_base = 500000.0
F32 = jnp.float32
BF16 = jnp.bfloat16
MIB = 2**20


def swap(a, axis):
    return lax.ppermute(a, axis, [(0, 1), (1, 0)])


def step_x(a):
    pairs = []
    for x in range(4):
        pairs.append((2 * x, 2 * ((x + 1) % 4)))
        pairs.append((2 * x + 1, 2 * ((x - 1) % 4) + 1))
    return lax.ppermute(a, ("x", "core"), pairs)


def shift_z(a, step):
    return lax.ppermute(a, "z", [(i, (i + step) % 4) for i in range(4)])


def rows_of(*parts):
    return jnp.concatenate(parts, 0)


def tables(first, rows):
    half = HD // 2
    index = jnp.arange(half).astype(F32)
    inverse = jnp.exp(-math.log(rope_base) * 2.0 * index / HD)
    positions = first * rows + jnp.arange(rows)
    angle = positions.astype(F32)[:, None] * inverse[None, :]
    cosine, sine = jnp.cos(angle), jnp.sin(angle)
    return jnp.concatenate([cosine, cosine], -1), jnp.concatenate([-sine, sine], -1)


def pick_kernel(idx, in_ref, out_ref):
    out_ref[...] = in_ref[...]


def pick_columns(a, idx):
    rows, n = a.shape[0], idx.shape[0]
    return pl.pallas_call(
        pick_kernel,
        grid_spec=pltpu.PrefetchScalarGridSpec(
            num_scalar_prefetch=1,
            grid=(n,),
            in_specs=[pl.BlockSpec((rows, 512), lambda i, idx: (0, idx[i]))],
            out_specs=pl.BlockSpec((rows, 512), lambda i, idx: (0, i)),
        ),
        out_shape=jax.ShapeDtypeStruct((rows, n * 512), a.dtype),
        compiler_params=pltpu.CompilerParams(vmem_limit_bytes=16 * MIB),
        cost_estimate=pl.CostEstimate(flops=0, bytes_accessed=16 * MIB, transcendentals=0),
    )(idx, a)


def project_kernel(plan, has_acc, h_ref, *refs):
    out_ref = refs[-1]
    width = out_ref.shape[1]
    i = pl.program_id(0)

    @pl.when(i == 0)
    def _():
        out_ref[...] = refs[-2][...] if has_acc else jnp.zeros_like(out_ref)

    for k, (which, row, col) in enumerate(plan):

        @pl.when(i == k)
        def _(which=which, row=row, col=col):
            w = refs[which][row : row + 512, col : col + width]
            out_ref[...] += jnp.dot(h_ref[...], w, preferred_element_type=F32)


def project(h, first, pieces, width, acc=None):
    plan = []
    for which, (p, col) in enumerate(pieces):
        plan += [(which, row, col) for row in range(0, p.shape[0], 512)]
    rows = h.shape[0]
    whole = pl.BlockSpec(memory_space=pltpu.VMEM)
    extra = [] if acc is None else [acc]
    return pl.pallas_call(
        functools.partial(project_kernel, tuple(plan), acc is not None),
        grid=(len(plan),),
        in_specs=[pl.BlockSpec((rows, 512), lambda i: (0, first + i))] + [whole] * (len(pieces) + len(extra)),
        out_specs=pl.BlockSpec((rows, width), lambda i: (0, 0)),
        out_shape=jax.ShapeDtypeStruct((rows, width), F32),
        compiler_params=pltpu.CompilerParams(vmem_limit_bytes=40 * MIB),
        cost_estimate=pl.CostEstimate(
            flops=2 * rows * 512 * width * len(plan), bytes_accessed=MIB * len(plan), transcendentals=0
        ),
    )(h, *[p for p, _ in pieces], *extra)


def attend_kernel(offset, idx, qa_ref, qb_ref, cos_ref, sin_ref, *refs):
    pieces, out_ref, kv_ref = refs[:-2], refs[-2], refs[-1]
    n = pl.program_id(0)

    @pl.when(n == 0)
    def _():
        at = 0
        for p in pieces:
            kv_ref[pl.ds(at, p.shape[0])] = p[...]
            at += p.shape[0]

    cosine, sine = cos_ref[...], sin_ref[...]
    heads = []
    for g in range(G):
        cols = slice(g * HD, (g + 1) * HD)
        t = qa_ref[:, cols] + qb_ref[:, cols]
        heads.append((t * cosine + pltpu.roll(t, HD // 2, 1) * sine).astype(BF16))
    q = jnp.concatenate(heads, 0)
    places = [pl.multiple_of(idx[offset + n, j] * BLOCK, BLOCK) for j in range(KB)]
    keys = jnp.concatenate([kv_ref[pl.ds(p, BLOCK), :HD] for p in places], 0)
    values = jnp.concatenate([kv_ref[pl.ds(p, BLOCK), HD:] for p in places], 0)
    s = lax.dot_general(q, keys, (((1,), (1,)), ((), ())), preferred_element_type=F32)
    top = jnp.max(s, -1, keepdims=True)
    e = jnp.exp2((s - top) * (math.log2(math.e) / math.sqrt(HD)))
    total = jnp.sum(e, -1, keepdims=True)
    o = jnp.dot(e.astype(BF16), values, preferred_element_type=F32) / total
    o = o.astype(BF16)
    for g in range(G):
        out_ref[:, g * HD : (g + 1) * HD] = o[g * BLOCK : (g + 1) * BLOCK]


def attend(seq, qa, qb, cosine, sine, pieces, idx, lblocks):
    first = seq * lblocks
    rows = sum(p.shape[0] for p in pieces)
    whole = pl.BlockSpec(memory_space=pltpu.VMEM)
    return pl.pallas_call(
        functools.partial(attend_kernel, first),
        grid_spec=pltpu.PrefetchScalarGridSpec(
            num_scalar_prefetch=1,
            grid=(lblocks,),
            in_specs=[
                pl.BlockSpec((BLOCK, G * HD), lambda n, idx: (first + n, 0)),
                pl.BlockSpec((BLOCK, G * HD), lambda n, idx: (first + n, 0)),
                pl.BlockSpec((BLOCK, HD), lambda n, idx: (n, 0)),
                pl.BlockSpec((BLOCK, HD), lambda n, idx: (n, 0)),
            ]
            + [whole] * len(pieces),
            out_specs=pl.BlockSpec((BLOCK, G * HD), lambda n, idx: (n, 0)),
            scratch_shapes=[pltpu.VMEM((rows, 2 * HD), BF16)],
        ),
        out_shape=jax.ShapeDtypeStruct((lblocks * BLOCK, G * HD), BF16),
        compiler_params=pltpu.CompilerParams(vmem_limit_bytes=48 * MIB),
        cost_estimate=pl.CostEstimate(flops=10**9, bytes_accessed=6 * MIB, transcendentals=2 * MIB),
    )(idx, qa, qb, cosine, sine, *pieces)


def mix_kernel(count, has_acc, idx, w_ref, *refs):
    out_ref = refs[-1]
    i = pl.program_id(0)

    @pl.when(i == 0)
    def _():
        out_ref[...] = refs[count][...] if has_acc else jnp.zeros_like(out_ref)

    for k in range(count):

        @pl.when(i == k)
        def _(k=k):
            out_ref[...] += jnp.dot(refs[k][...], w_ref[...], preferred_element_type=F32)


def mix(pieces, wo, idx, acc=None):
    rows, depth = pieces[0].shape
    n, width = len(pieces), wo.shape[1]
    whole = pl.BlockSpec(memory_space=pltpu.VMEM)
    extra = [] if acc is None else [acc]
    return pl.pallas_call(
        functools.partial(mix_kernel, n, acc is not None),
        grid_spec=pltpu.PrefetchScalarGridSpec(
            num_scalar_prefetch=1,
            grid=(n,),
            in_specs=[pl.BlockSpec((depth, width), lambda i, idx: (idx[i], 0))] + [whole] * (n + len(extra)),
            out_specs=pl.BlockSpec((rows, width), lambda i, idx: (0, 0)),
        ),
        out_shape=jax.ShapeDtypeStruct((rows, width), F32),
        compiler_params=pltpu.CompilerParams(vmem_limit_bytes=40 * MIB),
        cost_estimate=pl.CostEstimate(
            flops=2 * rows * n * depth * width, bytes_accessed=n * 3 * MIB, transcendentals=0
        ),
    )(idx, wo, *pieces, *extra)


def select(table, k):
    return sum(jnp.where(k == i, v, 0) for i, v in enumerate(table))


class Live(dict):

    def __getattr__(self, name):
        return self[name]

    def __setattr__(self, name, value):
        self[name] = value

    def sync(self):
        names = sorted(self)
        self.update(zip(names, lax.optimization_barrier([self[k] for k in names])))

    def drop(self, *names):
        for name in names:
            del self[name]


def on_device(hidden, wqkv, wo, picks):
    seqs, rows, feats = hidden.shape
    hidden = hidden.reshape(seqs * rows, feats)
    yh, x, core = lax.axis_index("yh"), lax.axis_index("x"), lax.axis_index("core")
    z, yl = lax.axis_index("z"), lax.axis_index("yl")
    lblocks = rows // BLOCK
    first = (yh * 4 + x) * 2 + core
    cosine, sine = tables(first, rows)
    qn = G * HD

    def blocks(c):
        back = jnp.where(c == 0, x + 3, x + 1) % 4
        out = []
        for a in range(2):
            for xx, cc in ((x, c), (back, c), (back, 1 - c), ((x + 2) % 4, c)):
                out.append(((yh ^ a) * 4 + xx) * 2 + cc)
        return jnp.stack(out).astype(jnp.int32)

    def slot_of(yy, xx, cc):
        turn = jnp.where(core == 0, xx - x, x - xx) % 4
        table = (0, 1, 11, 10, 4, 14, 2, 3, 5, 6, 13, 12, 9, 15, 7, 8)
        return select(table, (yy ^ yh) * 8 + turn * 2 + (cc ^ core))

    mine = lax.dynamic_slice_in_dim(picks, first * lblocks, lblocks, 1)
    owner, sub = mine // lblocks, mine % lblocks
    seq = jnp.arange(seqs)[:, None, None]
    idx = slot_of(owner // 8, (owner // 2) % 4, owner % 2) * (seqs * lblocks) + seq * lblocks + sub
    idx = idx.reshape(seqs * lblocks, KB).astype(jnp.int32)

    v = Live(w=wqkv, wo=wo)
    v.w_c = swap(v.w, "core")
    v.kv_y = swap(v.w[:, qn:], "yh")
    v.h_send = pick_columns(hidden, blocks(1 - core))
    v.sync()
    v.w_n = step_x(rows_of(v.w, v.w_c))
    v.q_y = swap(v.w[:, :qn], "yh")
    v.kv_yc = swap(v.kv_y, "core")
    v.h_own = pick_columns(hidden, blocks(core))
    v.h_part = swap(v.h_send, "core")
    v.drop("h_send")
    v.sync()
    v.kv_m = step_x(rows_of(v.kv_y, v.kv_yc))
    v.w_f = step_x(v.w_n[:512])
    v.q_yc = swap(v.q_y, "core")
    v.sync()
    v.kv_g = step_x(v.kv_m[:512])
    q_m = step_x(rows_of(v.q_y, v.q_yc))
    wo_all = lax.all_gather(v.wo, ("yh", "x", "core"), axis=0, tiled=True)
    v.drop("wo")
    v.sync()
    kv_pieces = [(v.w, qn), (v.w_n, qn), (v.w_f, qn), (v.kv_y, 0), (v.kv_m, 0), (v.kv_g, 0)]
    v.kv_got = swap(project(v.h_part, 0, kv_pieces, 2 * HD), "core")
    v.kv_own = project(v.h_own, 0, kv_pieces, 2 * HD)
    v.sync()
    kv = v.kv_own + v.kv_got
    keys = kv[:, :HD].reshape(seqs, rows, HD)
    keys = keys * cosine + jnp.roll(keys, HD // 2, -1) * sine
    v.p = jnp.concatenate([keys.reshape(seqs * rows, HD), kv[:, HD:]], -1).astype(BF16)
    v.p_c = swap(v.p, "core")
    v.p_y = swap(v.p, "yh")
    v.sync()
    v.p_n = step_x(rows_of(v.p, v.p_c))
    v.p_yc = swap(v.p_y, "core")
    v.q_m = q_m
    v.sync()
    v.p_m = step_x(rows_of(v.p_y, v.p_yc))
    v.p_f = step_x(v.p_n[:512])
    q_g = step_x(v.q_m[:512])
    q_pieces = [(v.w, 0), (v.w_n, 0), (v.w_f, 0), (v.q_y, 0), (v.q_m, 0)]
    v.q_part = project(v.h_part, 0, q_pieces, qn)
    v.sync()
    v.p_g = step_x(v.p_m[:512])
    v.p_b = swap(rows_of(v.p_n, v.p_m), "core")
    v.q_g = q_g
    v.q_own = project(v.h_own, 0, q_pieces, qn)
    v.sync()
    v.p_d = swap(rows_of(v.p_f, v.p_g), "core")
    v.q_got = swap(project(v.h_part, 7, [(v.q_g, 0)], qn, v.q_part), "core")
    v.q_own = project(v.h_own, 7, [(v.q_g, 0)], qn, v.q_own)
    v.sync()
    pieces = [v.p, v.p_c, v.p_n, v.p_f, v.p_y, v.p_yc, v.p_m, v.p_g, v.p_b, v.p_d]
    v = Live(
        s0=attend(0, v.q_own, v.q_got, cosine, sine, pieces, idx, lblocks),
        s1=attend(1, v.q_own, v.q_got, cosine, sine, pieces, idx, lblocks),
    )
    v.a_y = swap(v.s0, "yl")
    v.a_l, v.a_r = shift_z(v.s0, 1), shift_z(v.s0, -1)
    v.b_l, v.b_r = shift_z(v.s1, 1), shift_z(v.s1, -1)
    v.b_y = swap(v.s1, "yl")
    v.sync()
    v.a_yl, v.a_yr = shift_z(v.a_y, 1), shift_z(v.a_y, -1)
    v.a_f = shift_z(v.a_l, 1)
    v.b_f = shift_z(v.b_r, -1)
    v.b_ly, v.b_ry = swap(v.b_l, "yl"), swap(v.b_r, "yl")
    v.sync()
    v.a_yf = shift_z(v.a_yl, 1)
    v.b_fy = swap(v.b_f, "yl")

    def group(*at):
        return jnp.stack([((z + d) % 4) * 2 + (yl ^ a) for a, d in at]).astype(jnp.int32)

    near = group((0, 0), (0, 3), (0, 1), (1, 0))
    late = group((1, 3), (1, 1), (0, 2))
    last = group((1, 2))
    v.t0 = mix([v.s0, v.a_l, v.a_r, v.a_y], wo_all, near)
    v.t1 = mix([v.s1, v.b_l, v.b_r, v.b_y], wo_all, near)
    v.t0 = mix([v.a_yl, v.a_yr, v.a_f], wo_all, late, v.t0)
    v.t1 = mix([v.b_ly, v.b_ry, v.b_f], wo_all, late, v.t1)
    v.sync()
    t0 = mix([v.a_yf], wo_all, last, v.t0)
    t1 = mix([v.b_fy], wo_all, last, v.t1)
    return jnp.stack([t0, t1]).astype(BF16)


def solution(mesh):
    fine = Mesh(mesh.devices.reshape(2, 4, 2, 4, 2), ("yh", "x", "core", "z", "yl"))
    row, col = ("yh", "x", "core"), ("z", "yl")
    return jax.shard_map(
        on_device,
        mesh=fine,
        in_specs=(P(None, row, None), P(row, col), P(row, col), P()),
        out_specs=P(None, row, col),
        check_vma=False,
    )
```

```python
import functools
import math

import jax
import jax.numpy as jnp
from jax import lax
from jax.experimental import pallas as pl
from jax.experimental.pallas import tpu as pltpu
from jax.sharding import Mesh
from jax.sharding import PartitionSpec as P

HD = 128
BLOCK = 128
KB = 8
G = 8
HALF = G // 2
rope_base = 500000.0
F32 = jnp.float32
BF16 = jnp.bfloat16
MIB = 2**20


def swap(a, axis):
    return lax.ppermute(a, axis, [(0, 1), (1, 0)])


def step_x(a):
    pairs = []
    for x in range(4):
        pairs.append((2 * x, 2 * ((x + 1) % 4)))
        pairs.append((2 * x + 1, 2 * ((x - 1) % 4) + 1))
    return lax.ppermute(a, ("x", "core"), pairs)


def shift_z(a, step):
    return lax.ppermute(a, "z", [(i, (i + step) % 4) for i in range(4)])


def rows_of(*parts):
    return jnp.concatenate(parts, 0)


def tables(first, rows):
    half = HD // 2
    index = jnp.arange(half).astype(F32)
    inverse = jnp.exp(-math.log(rope_base) * 2.0 * index / HD)
    positions = first * rows + jnp.arange(rows)
    angle = positions.astype(F32)[:, None] * inverse[None, :]
    cosine, sine = jnp.cos(angle), jnp.sin(angle)
    return jnp.concatenate([cosine, cosine], -1), jnp.concatenate([-sine, sine], -1)


def pick_kernel(idx, in_ref, out_ref):
    out_ref[...] = in_ref[...]


def pick_columns(a, idx):
    rows, n = a.shape[0], idx.shape[0]
    return pl.pallas_call(
        pick_kernel,
        grid_spec=pltpu.PrefetchScalarGridSpec(
            num_scalar_prefetch=1,
            grid=(n,),
            in_specs=[pl.BlockSpec((rows, 512), lambda i, idx: (0, idx[i]))],
            out_specs=pl.BlockSpec((rows, 512), lambda i, idx: (0, i)),
        ),
        out_shape=jax.ShapeDtypeStruct((rows, n * 512), a.dtype),
        compiler_params=pltpu.CompilerParams(vmem_limit_bytes=16 * MIB),
        cost_estimate=pl.CostEstimate(flops=0, bytes_accessed=16 * MIB, transcendentals=0),
    )(idx, a)


def project_kernel(cols, part_h, own_h, *refs):
    n = len(cols)
    pieces, (part_ref, own_ref, h_ref, w_ref, sem) = refs[:n], refs[n:]
    rows, width = part_ref.shape
    copies = []
    for k in range(n):
        at = pl.ds(k * 512, 512)
        copies.append(
            (
                pltpu.make_async_copy(pieces[k].at[:, pl.ds(cols[k], width)], w_ref.at[at], sem.at[k, 0]),
                pltpu.make_async_copy(part_h.at[:, at], h_ref.at[pl.ds(0, rows), at], sem.at[k, 1]),
                pltpu.make_async_copy(own_h.at[:, at], h_ref.at[pl.ds(rows, rows), at], sem.at[k, 2]),
            )
        )
        for copy in copies[-1]:
            copy.start()
    for k in range(0, n, 2):
        for copy in copies[k] + copies[k + 1]:
            copy.wait()
        at = slice(k * 512, (k + 2) * 512)
        t = jnp.dot(h_ref[:, at], w_ref[at], preferred_element_type=F32)
        if k == 0:
            part_ref[...], own_ref[...] = t[:rows], t[rows:]
        else:
            part_ref[...] += t[:rows]
            own_ref[...] += t[rows:]


def project(h_part, h_own, pieces, width):
    n, rows = len(pieces), h_part.shape[0]
    away, whole = pl.BlockSpec(memory_space=pltpu.HBM), pl.BlockSpec(memory_space=pltpu.VMEM)
    return pl.pallas_call(
        functools.partial(project_kernel, tuple(col for _, col in pieces)),
        in_specs=[away] * (n + 2),
        out_specs=[whole] * 2,
        out_shape=[jax.ShapeDtypeStruct((rows, width), F32)] * 2,
        scratch_shapes=[
            pltpu.VMEM((2 * rows, n * 512), BF16),
            pltpu.VMEM((n * 512, width), BF16),
            pltpu.SemaphoreType.DMA((n, 3)),
        ],
        compiler_params=pltpu.CompilerParams(vmem_limit_bytes=32 * MIB),
        cost_estimate=pl.CostEstimate(
            flops=4 * rows * n * 512 * width, bytes_accessed=12 * MIB, transcendentals=0
        ),
    )(h_part, h_own, *[p for p, _ in pieces])


def attend_kernel(offset, idx, q1a_ref, q1b_ref, q0a_ref, q0b_ref, cos_ref, sin_ref, *refs):
    pieces, out_ref, kv_ref, sem = refs[:-3], refs[-3], refs[-2], refs[-1]
    n = pl.program_id(0)

    @pl.when(n == 0)
    def _():
        at, copies = 0, []
        for k, p in enumerate(pieces):
            copies.append(pltpu.make_async_copy(p, kv_ref.at[pl.ds(at, p.shape[0])], sem.at[k]))
            copies[-1].start()
            at += p.shape[0]
        for copy in copies:
            copy.wait()

    cosine, sine = cos_ref[...], sin_ref[...]
    heads = []
    for g in range(G):
        cols = slice(g % HALF * HD, (g % HALF + 1) * HD)
        one, two = (q1a_ref, q1b_ref) if g < HALF else (q0a_ref, q0b_ref)
        t = one[:, cols] + two[:, cols]
        heads.append((t * cosine + pltpu.roll(t, HD // 2, 1) * sine).astype(BF16))
    q = jnp.concatenate(heads, 0)
    places = [pl.multiple_of(idx[offset + n, j] * BLOCK, BLOCK) for j in range(KB)]
    keys = jnp.concatenate([kv_ref[pl.ds(p, BLOCK), :HD] for p in places], 0)
    values = jnp.concatenate([kv_ref[pl.ds(p, BLOCK), HD:] for p in places], 0)
    s = lax.dot_general(q, keys, (((1,), (1,)), ((), ())), preferred_element_type=F32)
    top = jnp.max(s, -1, keepdims=True)
    e = jnp.exp2((s - top) * (math.log2(math.e) / math.sqrt(HD)))
    total = jnp.sum(e, -1, keepdims=True)
    o = jnp.dot(e.astype(BF16), values, preferred_element_type=F32) / total
    o = o.astype(BF16)
    for g in range(G):
        out_ref[:, g * HD : (g + 1) * HD] = o[g * BLOCK : (g + 1) * BLOCK]


def attend(seq, queries, cosine, sine, pieces, idx, lblocks):
    first = seq * lblocks
    rows = sum(p.shape[0] for p in pieces)
    away = pl.BlockSpec(memory_space=pltpu.HBM)
    return pl.pallas_call(
        functools.partial(attend_kernel, first),
        grid_spec=pltpu.PrefetchScalarGridSpec(
            num_scalar_prefetch=1,
            grid=(lblocks,),
            in_specs=[
                pl.BlockSpec((BLOCK, HALF * HD), lambda n, idx: (first + n, 0)),
            ]
            * 4
            + [pl.BlockSpec((BLOCK, HD), lambda n, idx: (n, 0))] * 2
            + [away] * len(pieces),
            out_specs=pl.BlockSpec((BLOCK, G * HD), lambda n, idx: (n, 0)),
            scratch_shapes=[pltpu.VMEM((rows, 2 * HD), BF16), pltpu.SemaphoreType.DMA((len(pieces),))],
        ),
        out_shape=jax.ShapeDtypeStruct((lblocks * BLOCK, G * HD), BF16),
        compiler_params=pltpu.CompilerParams(vmem_limit_bytes=24 * MIB),
        cost_estimate=pl.CostEstimate(flops=10**9, bytes_accessed=6 * MIB, transcendentals=2 * MIB),
    )(idx, *queries, cosine, sine, *pieces)


def mix_kernel(count, idx, w_ref, *refs):
    acc_ref, out_ref = refs[-2:] if len(refs) == 2 * count + 2 else (None, refs[-1])
    i = pl.program_id(0)
    half = refs[0].shape[0]

    if count > 1:

        @pl.when(i == 0)
        def _():
            out_ref[...] = jnp.zeros_like(out_ref) if acc_ref is None else acc_ref[...]

        for k in range(count):

            @pl.when(i == k)
            def _(k=k):
                a = jnp.concatenate([refs[k][...], refs[count + k][...]], 0)
                out_ref[...] += jnp.dot(a, w_ref[...], preferred_element_type=F32)

    else:
        for k in range(2):
            rows = slice(k * half, (k + 1) * half)
            t = acc_ref[rows] + jnp.dot(refs[k][...], w_ref[...], preferred_element_type=F32)
            out_ref[rows] = t.astype(out_ref.dtype)


def mix(first, second, wo, idx, acc=None):
    rows, depth = first[0].shape
    n, width = len(first), wo.shape[1]
    whole = pl.BlockSpec(memory_space=pltpu.VMEM)
    extra = [] if acc is None else [acc]
    return pl.pallas_call(
        functools.partial(mix_kernel, n),
        grid_spec=pltpu.PrefetchScalarGridSpec(
            num_scalar_prefetch=1,
            grid=(n,),
            in_specs=[pl.BlockSpec((depth, width), lambda i, idx: (idx[i], 0))] + [whole] * (2 * n + len(extra)),
            out_specs=pl.BlockSpec((2 * rows, width), lambda i, idx: (0, 0)),
        ),
        out_shape=jax.ShapeDtypeStruct((2 * rows, width), F32 if n > 1 else BF16),
        compiler_params=pltpu.CompilerParams(vmem_limit_bytes=40 * MIB),
        cost_estimate=pl.CostEstimate(
            flops=4 * rows * n * depth * width, bytes_accessed=n * 3 * MIB, transcendentals=0
        ),
    )(idx, wo, *first, *second, *extra)


def select(table, k):
    return sum(jnp.where(k == i, v, 0) for i, v in enumerate(table))


class Live(dict):

    def __getattr__(self, name):
        return self[name]

    def __setattr__(self, name, value):
        self[name] = value

    def sync(self):
        names = sorted(self)
        self.update(zip(names, lax.optimization_barrier([self[k] for k in names])))

    def drop(self, *names):
        for name in names:
            del self[name]


def on_device(hidden, wqkv, wo, picks):
    seqs, rows, feats = hidden.shape
    hidden = hidden.reshape(seqs * rows, feats)
    yh, x, core = lax.axis_index("yh"), lax.axis_index("x"), lax.axis_index("core")
    z, yl = lax.axis_index("z"), lax.axis_index("yl")
    lblocks = rows // BLOCK
    first = (yh * 4 + x) * 2 + core
    cosine, sine = tables(first, rows)
    qn = G * HD

    def blocks(c):
        back = jnp.where(c == 0, x + 3, x + 1) % 4
        out = []
        for a in range(2):
            for xx, cc in ((x, c), (back, c), (back, 1 - c), ((x + 2) % 4, c)):
                out.append(((yh ^ a) * 4 + xx) * 2 + cc)
        return jnp.stack(out).astype(jnp.int32)

    def slot_of(yy, xx, cc):
        turn = jnp.where(core == 0, xx - x, x - xx) % 4
        table = (0, 1, 11, 10, 4, 14, 2, 3, 5, 6, 13, 12, 9, 15, 7, 8)
        return select(table, (yy ^ yh) * 8 + turn * 2 + (cc ^ core))

    mine = lax.dynamic_slice_in_dim(picks, first * lblocks, lblocks, 1)
    owner, sub = mine // lblocks, mine % lblocks
    seq = jnp.arange(seqs)[:, None, None]
    idx = slot_of(owner // 8, (owner // 2) % 4, owner % 2) * (seqs * lblocks) + seq * lblocks + sub
    idx = idx.reshape(seqs * lblocks, KB).astype(jnp.int32)

    v = Live(w=wqkv, wo=wo)
    qh = HALF * HD
    v.w_n = step_x(v.w)
    v.w_c = swap(v.w, "core")
    v.kv_y = swap(v.w[:, qn:], "yh")
    v.q1_y = swap(v.w[:, :qh], "yh")
    v.sync()
    v.w_m = step_x(v.w_c)
    v.kv_yn = step_x(v.kv_y)
    v.kv_yc, v.q1_yc = swap(v.kv_y, "core"), swap(v.q1_y, "core")
    v.q0_y = swap(v.w[:, qh:qn], "yh")
    v.h_send = pick_columns(hidden, blocks(1 - core))
    v.h_own = pick_columns(hidden, blocks(core))
    v.sync()
    v.kv_ym, v.kv_yf = step_x(v.kv_yc), step_x(v.kv_yn)
    v.w_f = step_x(v.w_n)
    v.q0_yn = swap(v.w_n[:, qh:qn], "yh")
    v.h_part = swap(v.h_send, "core")
    v.drop("h_send")
    v.sync()

    def pieces_of(name, col):
        ends = ("_y", "_yn", "_ym", "_yf")
        return [(v.w, col), (v.w_n, col), (v.w_m, col), (v.w_f, col)] + [(v[name + e], 0) for e in ends]

    wo_all = lax.all_gather(v.wo, ("yh", "x", "core"), axis=0, tiled=True)
    v.drop("wo")
    v.q1_yn, v.q1_ym = step_x(v.q1_y), step_x(v.q1_yc)
    v.q0_ym = swap(v.w_m[:, qh:qn], "yh")
    v.kv_part, v.kv_own = project(v.h_part, v.h_own, pieces_of("kv", qn), 2 * HD)
    v.sync()
    v.kv_got = swap(v.kv_part, "core")
    v.q1_yf = step_x(v.q1_yn)
    v.sync()
    kv = v.kv_own + v.kv_got
    keys = kv[:, :HD].reshape(seqs, rows, HD)
    keys = keys * cosine + jnp.roll(keys, HD // 2, -1) * sine
    v.p = jnp.concatenate([keys.reshape(seqs * rows, HD), kv[:, HD:]], -1).astype(BF16)
    v.p_n = step_x(v.p)
    v.p_c = swap(v.p, "core")
    v.p_y = swap(v.p, "yh")
    v.q1_part, v.q1_own = project(v.h_part, v.h_own, pieces_of("q1", 0), qh)
    v.sync()
    v.p_m, v.p_yn, v.p_f = step_x(v.p_c), step_x(v.p_y), step_x(v.p_n)
    v.p_yc = swap(v.p_y, "core")
    v.q0_yf = swap(v.w_f[:, qh:qn], "yh")
    v.q1_got = swap(v.q1_part, "core")
    v.sync()
    v.p_ym, v.p_yf = step_x(v.p_yc), step_x(v.p_yn)
    v.p_nc, v.p_mc, v.p_ync, v.p_fc = [swap(v["p_" + k], "core") for k in ("n", "m", "yn", "f")]
    v.q0_part, v.q0_own = project(v.h_part, v.h_own, pieces_of("q0", qh), qh)
    v.sync()
    v.q0_got = swap(v.q0_part, "core")
    v.p_ymc, v.p_yfc = swap(v.p_ym, "core"), swap(v.p_yf, "core")
    v.sync()
    ends = ("", "_c", "_n", "_m", "_f", "_y", "_yc", "_yn", "_ym", "_yf", "_nc", "_mc", "_ync", "_ymc", "_fc", "_yfc")
    pieces = [v["p" + e] for e in ends]
    queries = [v.q1_own, v.q1_got, v.q0_own, v.q0_got]
    def group(*at):
        return jnp.stack([((z + d) % 4) * 2 + (yl ^ a) for a, d in at]).astype(jnp.int32)

    v = Live(
        s0=attend(0, queries, cosine, sine, pieces, idx, lblocks),
        s1=attend(1, queries, cosine, sine, pieces, idx, lblocks),
    )
    v.a_y = swap(v.s0, "yl")
    v.a_l, v.a_r = shift_z(v.s0, 1), shift_z(v.s0, -1)
    v.b_l, v.b_r = shift_z(v.s1, 1), shift_z(v.s1, -1)
    v.b_y = swap(v.s1, "yl")
    v.sync()
    v.a_yl, v.a_yr = shift_z(v.a_y, 1), shift_z(v.a_y, -1)
    v.a_f = shift_z(v.a_l, 1)
    v.b_f = shift_z(v.b_r, -1)
    v.b_ly, v.b_ry = swap(v.b_l, "yl"), swap(v.b_r, "yl")
    v.t = mix([v.s0, v.a_l, v.a_r, v.a_y], [v.s1, v.b_l, v.b_r, v.b_y], wo_all, group((0, 0), (0, 3), (0, 1), (1, 0)))
    v.sync()
    v.a_yf = shift_z(v.a_yl, 1)
    v.b_fy = swap(v.b_f, "yl")

    late = group((1, 3), (1, 1), (0, 2))
    v.t = mix([v.a_yl, v.a_yr, v.a_f], [v.b_ly, v.b_ry, v.b_f], wo_all, late, v.t)
    v.sync()
    return mix([v.a_yf], [v.b_fy], wo_all, group((1, 2)), v.t).reshape(seqs, rows, wo.shape[1])


def solution(mesh):
    fine = Mesh(mesh.devices.reshape(2, 4, 2, 4, 2), ("yh", "x", "core", "z", "yl"))
    row, col = ("yh", "x", "core"), ("z", "yl")
    return jax.shard_map(
        on_device,
        mesh=fine,
        in_specs=(P(None, row, None), P(row, col), P(row, col), P()),
        out_specs=P(None, row, col),
        check_vma=False,
    )
```

```python
import functools
import math

import jax
import jax.numpy as jnp
from jax import lax
from jax.experimental import pallas as pl
from jax.experimental.pallas import tpu as pltpu
from jax.sharding import Mesh
from jax.sharding import PartitionSpec as P

HD = 128
BLOCK = 128
KB = 8
G = 8
HALF = G // 2
rope_base = 500000.0
F32 = jnp.float32
BF16 = jnp.bfloat16
MIB = 2**20


def swap(a, axis):
    return lax.ppermute(a, axis, [(0, 1), (1, 0)])


def step_x(a):
    pairs = []
    for x in range(4):
        pairs.append((2 * x, 2 * ((x + 1) % 4)))
        pairs.append((2 * x + 1, 2 * ((x - 1) % 4) + 1))
    return lax.ppermute(a, ("x", "core"), pairs)


def shift_z(a, step):
    return lax.ppermute(a, "z", [(i, (i + step) % 4) for i in range(4)])


def rows_of(*parts):
    return jnp.concatenate(parts, 0)


def tables(first, rows):
    half = HD // 2
    index = jnp.arange(half).astype(F32)
    inverse = jnp.exp(-math.log(rope_base) * 2.0 * index / HD)
    positions = first * rows + jnp.arange(rows)
    angle = positions.astype(F32)[:, None] * inverse[None, :]
    cosine, sine = jnp.cos(angle), jnp.sin(angle)
    return jnp.concatenate([cosine, cosine], -1), jnp.concatenate([-sine, sine], -1)


def pick_kernel(idx, in_ref, out_ref):
    out_ref[...] = in_ref[...]


def pick_columns(a, idx):
    rows, n = a.shape[0], idx.shape[0]
    return pl.pallas_call(
        pick_kernel,
        grid_spec=pltpu.PrefetchScalarGridSpec(
            num_scalar_prefetch=1,
            grid=(n,),
            in_specs=[pl.BlockSpec((rows, 512), lambda i, idx: (0, idx[i]))],
            out_specs=pl.BlockSpec((rows, 512), lambda i, idx: (0, i)),
        ),
        out_shape=jax.ShapeDtypeStruct((rows, n * 512), a.dtype),
        compiler_params=pltpu.CompilerParams(vmem_limit_bytes=16 * MIB),
        cost_estimate=pl.CostEstimate(flops=0, bytes_accessed=16 * MIB, transcendentals=0),
    )(idx, a)


def project_kernel(cols, part_h, own_h, *refs):
    n = len(cols)
    pieces, (part_ref, own_ref, h_ref, w_ref, sem) = refs[:n], refs[n:]
    rows, width = part_ref.shape
    copies = []
    for k in range(n):
        at = pl.ds(k * 512, 512)
        copies.append(
            (
                pltpu.make_async_copy(pieces[k].at[:, pl.ds(cols[k], width)], w_ref.at[at], sem.at[k, 0]),
                pltpu.make_async_copy(part_h.at[:, at], h_ref.at[pl.ds(0, rows), at], sem.at[k, 1]),
                pltpu.make_async_copy(own_h.at[:, at], h_ref.at[pl.ds(rows, rows), at], sem.at[k, 2]),
            )
        )
        for copy in copies[-1]:
            copy.start()
    for k in range(0, n, 2):
        for copy in copies[k] + copies[k + 1]:
            copy.wait()
        at = slice(k * 512, (k + 2) * 512)
        t = jnp.dot(h_ref[:, at], w_ref[at], preferred_element_type=F32)
        if k == 0:
            part_ref[...], own_ref[...] = t[:rows], t[rows:]
        else:
            part_ref[...] += t[:rows]
            own_ref[...] += t[rows:]


def project(h_part, h_own, pieces, width):
    n, rows = len(pieces), h_part.shape[0]
    away, whole = pl.BlockSpec(memory_space=pl.ANY), pl.BlockSpec(memory_space=pltpu.VMEM)
    return pl.pallas_call(
        functools.partial(project_kernel, tuple(col for _, col in pieces)),
        in_specs=[away] * (n + 2),
        out_specs=[whole] * 2,
        out_shape=[jax.ShapeDtypeStruct((rows, width), F32)] * 2,
        scratch_shapes=[
            pltpu.VMEM((2 * rows, n * 512), BF16),
            pltpu.VMEM((n * 512, width), BF16),
            pltpu.SemaphoreType.DMA((n, 3)),
        ],
        compiler_params=pltpu.CompilerParams(vmem_limit_bytes=60 * MIB),
        cost_estimate=pl.CostEstimate(
            flops=4 * rows * n * 512 * width, bytes_accessed=12 * MIB, transcendentals=0
        ),
    )(h_part, h_own, *[p for p, _ in pieces])


def attend_kernel(offset, idx, q1a_ref, q1b_ref, q0a_ref, q0b_ref, cos_ref, sin_ref, *refs):
    pieces, out_ref, kv_ref, sem = refs[:-3], refs[-3], refs[-2], refs[-1]
    n = pl.program_id(0)

    @pl.when(n == 0)
    def _():
        at, copies = 0, []
        for k, p in enumerate(pieces):
            copies.append(pltpu.make_async_copy(p, kv_ref.at[pl.ds(at, p.shape[0])], sem.at[k]))
            copies[-1].start()
            at += p.shape[0]
        for copy in copies:
            copy.wait()

    cosine, sine = cos_ref[...], sin_ref[...]
    heads = []
    for g in range(G):
        cols = slice(g % HALF * HD, (g % HALF + 1) * HD)
        one, two = (q1a_ref, q1b_ref) if g < HALF else (q0a_ref, q0b_ref)
        t = one[:, cols] + two[:, cols]
        heads.append((t * cosine + pltpu.roll(t, HD // 2, 1) * sine).astype(BF16))
    q = jnp.concatenate(heads, 0)
    places = [pl.multiple_of(idx[offset + n, j] * BLOCK, BLOCK) for j in range(KB)]
    keys = jnp.concatenate([kv_ref[pl.ds(p, BLOCK), :HD] for p in places], 0)
    values = jnp.concatenate([kv_ref[pl.ds(p, BLOCK), HD:] for p in places], 0)
    s = lax.dot_general(q, keys, (((1,), (1,)), ((), ())), preferred_element_type=F32)
    top = jnp.max(s, -1, keepdims=True)
    e = jnp.exp2((s - top) * (math.log2(math.e) / math.sqrt(HD)))
    total = jnp.sum(e, -1, keepdims=True)
    o = jnp.dot(e.astype(BF16), values, preferred_element_type=F32) / total
    o = o.astype(BF16)
    for g in range(G):
        out_ref[:, g * HD : (g + 1) * HD] = o[g * BLOCK : (g + 1) * BLOCK]


def attend(seq, queries, cosine, sine, pieces, idx, lblocks):
    first = seq * lblocks
    rows = sum(p.shape[0] for p in pieces)
    away = pl.BlockSpec(memory_space=pl.ANY)
    return pl.pallas_call(
        functools.partial(attend_kernel, first),
        grid_spec=pltpu.PrefetchScalarGridSpec(
            num_scalar_prefetch=1,
            grid=(lblocks,),
            in_specs=[
                pl.BlockSpec((BLOCK, HALF * HD), lambda n, idx: (first + n, 0)),
            ]
            * 4
            + [pl.BlockSpec((BLOCK, HD), lambda n, idx: (n, 0))] * 2
            + [away] * len(pieces),
            out_specs=pl.BlockSpec((BLOCK, G * HD), lambda n, idx: (n, 0)),
            scratch_shapes=[pltpu.VMEM((rows, 2 * HD), BF16), pltpu.SemaphoreType.DMA((len(pieces),))],
        ),
        out_shape=jax.ShapeDtypeStruct((lblocks * BLOCK, G * HD), BF16),
        compiler_params=pltpu.CompilerParams(vmem_limit_bytes=60 * MIB),
        cost_estimate=pl.CostEstimate(flops=10**9, bytes_accessed=6 * MIB, transcendentals=2 * MIB),
    )(idx, *queries, cosine, sine, *pieces)


def mix_kernel(count, idx, w_ref, *refs):
    acc_ref, out_ref = refs[-2:] if len(refs) == 2 * count + 2 else (None, refs[-1])
    i = pl.program_id(0)
    half = refs[0].shape[0]

    if count > 1:

        @pl.when(i == 0)
        def _():
            out_ref[...] = jnp.zeros_like(out_ref) if acc_ref is None else acc_ref[...]

        for k in range(count):

            @pl.when(i == k)
            def _(k=k):
                a = jnp.concatenate([refs[k][...], refs[count + k][...]], 0)
                out_ref[...] += jnp.dot(a, w_ref[...], preferred_element_type=F32)

    else:
        for k in range(2):
            rows = slice(k * half, (k + 1) * half)
            t = acc_ref[rows] + jnp.dot(refs[k][...], w_ref[...], preferred_element_type=F32)
            out_ref[rows] = t.astype(out_ref.dtype)


def mix(first, second, wo, idx, acc=None):
    rows, depth = first[0].shape
    n, width = len(first), wo.shape[1]
    whole = pl.BlockSpec(memory_space=pltpu.VMEM)
    extra = [] if acc is None else [acc]
    return pl.pallas_call(
        functools.partial(mix_kernel, n),
        grid_spec=pltpu.PrefetchScalarGridSpec(
            num_scalar_prefetch=1,
            grid=(n,),
            in_specs=[pl.BlockSpec((depth, width), lambda i, idx: (idx[i], 0))] + [whole] * (2 * n + len(extra)),
            out_specs=pl.BlockSpec((2 * rows, width), lambda i, idx: (0, 0)),
        ),
        out_shape=jax.ShapeDtypeStruct((2 * rows, width), F32 if n > 1 else BF16),
        compiler_params=pltpu.CompilerParams(vmem_limit_bytes=40 * MIB),
        cost_estimate=pl.CostEstimate(
            flops=4 * rows * n * depth * width, bytes_accessed=n * 3 * MIB, transcendentals=0
        ),
    )(idx, wo, *first, *second, *extra)


def select(table, k):
    return sum(jnp.where(k == i, v, 0) for i, v in enumerate(table))


class Live(dict):

    def __getattr__(self, name):
        return self[name]

    def __setattr__(self, name, value):
        self[name] = value

    def sync(self):
        names = sorted(self)
        self.update(zip(names, lax.optimization_barrier([self[k] for k in names])))

    def drop(self, *names):
        for name in names:
            del self[name]


def on_device(hidden, wqkv, wo, picks):
    seqs, rows, feats = hidden.shape
    hidden = hidden.reshape(seqs * rows, feats)
    yh, x, core = lax.axis_index("yh"), lax.axis_index("x"), lax.axis_index("core")
    z, yl = lax.axis_index("z"), lax.axis_index("yl")
    lblocks = rows // BLOCK
    first = (yh * 4 + x) * 2 + core
    cosine, sine = tables(first, rows)
    qn = G * HD

    def blocks(c):
        back = jnp.where(c == 0, x + 3, x + 1) % 4
        out = []
        for a in range(2):
            for xx, cc in ((x, c), (back, c), (back, 1 - c), ((x + 2) % 4, c)):
                out.append(((yh ^ a) * 4 + xx) * 2 + cc)
        return jnp.stack(out).astype(jnp.int32)

    def slot_of(yy, xx, cc):
        turn = jnp.where(core == 0, xx - x, x - xx) % 4
        table = (0, 1, 11, 10, 4, 14, 2, 3, 5, 6, 13, 12, 9, 15, 7, 8)
        return select(table, (yy ^ yh) * 8 + turn * 2 + (cc ^ core))

    mine = lax.dynamic_slice_in_dim(picks, first * lblocks, lblocks, 1)
    owner, sub = mine // lblocks, mine % lblocks
    seq = jnp.arange(seqs)[:, None, None]
    idx = slot_of(owner // 8, (owner // 2) % 4, owner % 2) * (seqs * lblocks) + seq * lblocks + sub
    idx = idx.reshape(seqs * lblocks, KB).astype(jnp.int32)

    v = Live(w=wqkv, wo=wo)
    qh = HALF * HD
    v.w_n = step_x(v.w)
    v.w_c = swap(v.w, "core")
    v.kv_y = swap(v.w[:, qn:], "yh")
    v.q1_y = swap(v.w[:, :qh], "yh")
    v.sync()
    v.w_m = step_x(v.w_c)
    v.kv_yn = step_x(v.kv_y)
    v.kv_yc, v.q1_yc = swap(v.kv_y, "core"), swap(v.q1_y, "core")
    v.q0_y = swap(v.w[:, qh:qn], "yh")
    v.h_send = pick_columns(hidden, blocks(1 - core))
    v.h_own = pick_columns(hidden, blocks(core))
    v.sync()
    v.kv_ym, v.kv_yf = step_x(v.kv_yc), step_x(v.kv_yn)
    v.w_f = step_x(v.w_n)
    v.q0_yn = swap(v.w_n[:, qh:qn], "yh")
    v.h_part = swap(v.h_send, "core")
    v.drop("h_send")
    v.sync()

    def pieces_of(name, col):
        ends = ("_y", "_yn", "_ym", "_yf")
        return [(v.w, col), (v.w_n, col), (v.w_m, col), (v.w_f, col)] + [(v[name + e], 0) for e in ends]

    v.q1_yn, v.q1_ym = step_x(v.q1_y), step_x(v.q1_yc)
    v.q0_ym = swap(v.w_m[:, qh:qn], "yh")
    v.kv_part, v.kv_own = project(v.h_part, v.h_own, pieces_of("kv", qn), 2 * HD)
    v.sync()
    wo_all = lax.all_gather(v.wo, ("yh", "x", "core"), axis=0, tiled=True)
    v.drop("wo")
    v.kv_got = swap(v.kv_part, "core")
    v.q1_yf = step_x(v.q1_yn)
    v.sync()
    kv = v.kv_own + v.kv_got
    keys = kv[:, :HD].reshape(seqs, rows, HD)
    keys = keys * cosine + jnp.roll(keys, HD // 2, -1) * sine
    v.p = jnp.concatenate([keys.reshape(seqs * rows, HD), kv[:, HD:]], -1).astype(BF16)
    v.p_n = step_x(v.p)
    v.p_c = swap(v.p, "core")
    v.p_y = swap(v.p, "yh")
    v.q1_part, v.q1_own = project(v.h_part, v.h_own, pieces_of("q1", 0), qh)
    v.sync()
    v.p_m, v.p_yn, v.p_f = step_x(v.p_c), step_x(v.p_y), step_x(v.p_n)
    v.p_yc = swap(v.p_y, "core")
    v.q0_yf = swap(v.w_f[:, qh:qn], "yh")
    v.q1_got = swap(v.q1_part, "core")
    v.sync()
    v.p_ym, v.p_yf = step_x(v.p_yc), step_x(v.p_yn)
    v.p_nc, v.p_mc, v.p_ync, v.p_fc = [swap(v["p_" + k], "core") for k in ("n", "m", "yn", "f")]
    v.q0_part, v.q0_own = project(v.h_part, v.h_own, pieces_of("q0", qh), qh)
    v.sync()
    v.q0_got = swap(v.q0_part, "core")
    v.p_ymc, v.p_yfc = swap(v.p_ym, "core"), swap(v.p_yf, "core")
    v.sync()
    ends = ("", "_c", "_n", "_m", "_f", "_y", "_yc", "_yn", "_ym", "_yf", "_nc", "_mc", "_ync", "_ymc", "_fc", "_yfc")
    pieces = [v["p" + e] for e in ends]
    queries = [v.q1_own, v.q1_got, v.q0_own, v.q0_got]
    def group(*at):
        return jnp.stack([((z + d) % 4) * 2 + (yl ^ a) for a, d in at]).astype(jnp.int32)

    v = Live(
        s0=attend(0, queries, cosine, sine, pieces, idx, lblocks),
        s1=attend(1, queries, cosine, sine, pieces, idx, lblocks),
    )
    v.a_y = swap(v.s0, "yl")
    v.a_l, v.a_r = shift_z(v.s0, 1), shift_z(v.s0, -1)
    v.b_l, v.b_r = shift_z(v.s1, 1), shift_z(v.s1, -1)
    v.b_y = swap(v.s1, "yl")
    v.sync()
    v.a_yl, v.a_yr = shift_z(v.a_y, 1), shift_z(v.a_y, -1)
    v.a_f = shift_z(v.a_l, 1)
    v.b_f = shift_z(v.b_r, -1)
    v.b_ly, v.b_ry = swap(v.b_l, "yl"), swap(v.b_r, "yl")
    v.t = mix([v.s0, v.a_l, v.a_r, v.a_y], [v.s1, v.b_l, v.b_r, v.b_y], wo_all, group((0, 0), (0, 3), (0, 1), (1, 0)))
    v.sync()
    v.a_yf = shift_z(v.a_yl, 1)
    v.b_fy = swap(v.b_f, "yl")

    late = group((1, 3), (1, 1), (0, 2))
    v.t = mix([v.a_yl, v.a_yr, v.a_f], [v.b_ly, v.b_ry, v.b_f], wo_all, late, v.t)
    v.sync()
    return mix([v.a_yf], [v.b_fy], wo_all, group((1, 2)), v.t).reshape(seqs, rows, wo.shape[1])


def solution(mesh):
    fine = Mesh(mesh.devices.reshape(2, 4, 2, 4, 2), ("yh", "x", "core", "z", "yl"))
    row, col = ("yh", "x", "core"), ("z", "yl")
    return jax.shard_map(
        on_device,
        mesh=fine,
        in_specs=(P(None, row, None), P(row, col), P(row, col), P()),
        out_specs=P(None, row, col),
        check_vma=False,
    )
```

```python
import functools
import math

import jax
import jax.numpy as jnp
from jax import lax
from jax.experimental import pallas as pl
from jax.experimental.pallas import tpu as pltpu
from jax.sharding import Mesh
from jax.sharding import PartitionSpec as P

HD = 128
BLOCK = 128
KB = 8
G = 8
HALF = G // 2
rope_base = 500000.0
F32 = jnp.float32
BF16 = jnp.bfloat16
MIB = 2**20


def swap(a, axis):
    return lax.ppermute(a, axis, [(0, 1), (1, 0)])


def step_x(a):
    pairs = []
    for x in range(4):
        pairs.append((2 * x, 2 * ((x + 1) % 4)))
        pairs.append((2 * x + 1, 2 * ((x - 1) % 4) + 1))
    return lax.ppermute(a, ("x", "core"), pairs)


def shift_z(a, step):
    return lax.ppermute(a, "z", [(i, (i + step) % 4) for i in range(4)])


def rows_of(*parts):
    return jnp.concatenate(parts, 0)


def tables(first, rows):
    half = HD // 2
    index = jnp.arange(half).astype(F32)
    inverse = jnp.exp(-math.log(rope_base) * 2.0 * index / HD)
    positions = first * rows + jnp.arange(rows)
    angle = positions.astype(F32)[:, None] * inverse[None, :]
    cosine, sine = jnp.cos(angle), jnp.sin(angle)
    return jnp.concatenate([cosine, cosine], -1), jnp.concatenate([-sine, sine], -1)


def pick_kernel(idx, in_ref, out_ref):
    out_ref[...] = in_ref[...]


def pick_columns(a, idx):
    rows, n = a.shape[0], idx.shape[0]
    return pl.pallas_call(
        pick_kernel,
        grid_spec=pltpu.PrefetchScalarGridSpec(
            num_scalar_prefetch=1,
            grid=(n,),
            in_specs=[pl.BlockSpec((rows, 512), lambda i, idx: (0, idx[i]))],
            out_specs=pl.BlockSpec((rows, 512), lambda i, idx: (0, i)),
        ),
        out_shape=jax.ShapeDtypeStruct((rows, n * 512), a.dtype),
        compiler_params=pltpu.CompilerParams(vmem_limit_bytes=16 * MIB),
        cost_estimate=pl.CostEstimate(flops=0, bytes_accessed=16 * MIB, transcendentals=0),
    )(idx, a)


def project_kernel(cols, part_h, own_h, *refs):
    n = len(cols)
    pieces, (part_ref, own_ref, h_ref, w_ref, sem) = refs[:n], refs[n:]
    rows, width = part_ref.shape
    copies = []
    for k in range(n):
        at = pl.ds(k * 512, 512)
        copies.append(
            (
                pltpu.make_async_copy(pieces[k].at[:, pl.ds(cols[k], width)], w_ref.at[at], sem.at[k, 0]),
                pltpu.make_async_copy(part_h.at[:, at], h_ref.at[pl.ds(0, rows), at], sem.at[k, 1]),
                pltpu.make_async_copy(own_h.at[:, at], h_ref.at[pl.ds(rows, rows), at], sem.at[k, 2]),
            )
        )
        for copy in copies[-1]:
            copy.start()
    for k in range(0, n, 2):
        for copy in copies[k] + copies[k + 1]:
            copy.wait()
        at = slice(k * 512, (k + 2) * 512)
        t = jnp.dot(h_ref[:, at], w_ref[at], preferred_element_type=F32)
        if k == 0:
            part_ref[...], own_ref[...] = t[:rows], t[rows:]
        else:
            part_ref[...] += t[:rows]
            own_ref[...] += t[rows:]


def project(h_part, h_own, pieces, width):
    n, rows = len(pieces), h_part.shape[0]
    away, whole = pl.BlockSpec(memory_space=pl.ANY), pl.BlockSpec(memory_space=pltpu.VMEM)
    return pl.pallas_call(
        functools.partial(project_kernel, tuple(col for _, col in pieces)),
        in_specs=[away] * (n + 2),
        out_specs=[whole] * 2,
        out_shape=[jax.ShapeDtypeStruct((rows, width), F32)] * 2,
        scratch_shapes=[
            pltpu.VMEM((2 * rows, n * 512), BF16),
            pltpu.VMEM((n * 512, width), BF16),
            pltpu.SemaphoreType.DMA((n, 3)),
        ],
        compiler_params=pltpu.CompilerParams(vmem_limit_bytes=60 * MIB),
        cost_estimate=pl.CostEstimate(
            flops=4 * rows * n * 512 * width, bytes_accessed=12 * MIB, transcendentals=0
        ),
    )(h_part, h_own, *[p for p, _ in pieces])


def attend_kernel(offset, idx, q1a_ref, q1b_ref, q0a_ref, q0b_ref, cos_ref, sin_ref, *refs):
    pieces, out_ref, kv_ref, sem = refs[:-3], refs[-3], refs[-2], refs[-1]
    n = pl.program_id(0)

    @pl.when(n == 0)
    def _():
        at, copies = 0, []
        for k, p in enumerate(pieces):
            copies.append(pltpu.make_async_copy(p, kv_ref.at[pl.ds(at, p.shape[0])], sem.at[k]))
            copies[-1].start()
            at += p.shape[0]
        for copy in copies:
            copy.wait()

    cosine, sine = cos_ref[...], sin_ref[...]
    heads = []
    for g in range(G):
        cols = slice(g % HALF * HD, (g % HALF + 1) * HD)
        one, two = (q1a_ref, q1b_ref) if g < HALF else (q0a_ref, q0b_ref)
        t = one[:, cols] + two[:, cols]
        heads.append((t * cosine + pltpu.roll(t, HD // 2, 1) * sine).astype(BF16))
    q = jnp.concatenate(heads, 0)
    places = [pl.multiple_of(idx[offset + n, j] * BLOCK, BLOCK) for j in range(KB)]
    keys = jnp.concatenate([kv_ref[pl.ds(p, BLOCK), :HD] for p in places], 0)
    values = jnp.concatenate([kv_ref[pl.ds(p, BLOCK), HD:] for p in places], 0)
    s = lax.dot_general(q, keys, (((1,), (1,)), ((), ())), preferred_element_type=F32)
    top = jnp.max(s, -1, keepdims=True)
    e = jnp.exp2((s - top) * (math.log2(math.e) / math.sqrt(HD)))
    total = jnp.sum(e, -1, keepdims=True)
    o = jnp.dot(e.astype(BF16), values, preferred_element_type=F32) / total
    o = o.astype(BF16)
    for g in range(G):
        out_ref[:, g * HD : (g + 1) * HD] = o[g * BLOCK : (g + 1) * BLOCK]


def attend(seq, queries, cosine, sine, pieces, idx, lblocks):
    first = seq * lblocks
    rows = sum(p.shape[0] for p in pieces)
    away = pl.BlockSpec(memory_space=pl.ANY)
    return pl.pallas_call(
        functools.partial(attend_kernel, first),
        grid_spec=pltpu.PrefetchScalarGridSpec(
            num_scalar_prefetch=1,
            grid=(lblocks,),
            in_specs=[
                pl.BlockSpec((BLOCK, HALF * HD), lambda n, idx: (first + n, 0)),
            ]
            * 4
            + [pl.BlockSpec((BLOCK, HD), lambda n, idx: (n, 0))] * 2
            + [away] * len(pieces),
            out_specs=pl.BlockSpec((BLOCK, G * HD), lambda n, idx: (n, 0)),
            scratch_shapes=[pltpu.VMEM((rows, 2 * HD), BF16), pltpu.SemaphoreType.DMA((len(pieces),))],
        ),
        out_shape=jax.ShapeDtypeStruct((lblocks * BLOCK, G * HD), BF16),
        compiler_params=pltpu.CompilerParams(vmem_limit_bytes=60 * MIB),
        cost_estimate=pl.CostEstimate(flops=10**9, bytes_accessed=6 * MIB, transcendentals=2 * MIB),
    )(idx, *queries, cosine, sine, *pieces)


def mix_kernel(count, idx, w_ref, *refs):
    acc_ref, out_ref = refs[-2:] if len(refs) == 2 * count + 2 else (None, refs[-1])
    i = pl.program_id(0)
    half, depth = refs[0].shape
    w = w_ref[0, :, 0].reshape(depth, w_ref.shape[-1])

    if count > 1:

        @pl.when(i == 0)
        def _():
            out_ref[...] = jnp.zeros_like(out_ref) if acc_ref is None else acc_ref[...]

        for k in range(count):

            @pl.when(i == k)
            def _(k=k):
                a = jnp.concatenate([refs[k][...], refs[count + k][...]], 0)
                out_ref[...] += jnp.dot(a, w, preferred_element_type=F32)

    else:
        for k in range(2):
            rows = slice(k * half, (k + 1) * half)
            t = acc_ref[rows] + jnp.dot(refs[k][...], w, preferred_element_type=F32)
            out_ref[rows] = t.astype(out_ref.dtype)


def mix(first, second, wo, idx, acc=None):
    rows, depth = first[0].shape
    n, width = len(first), wo.shape[-1]
    whole = pl.BlockSpec(memory_space=pltpu.VMEM)
    extra = [] if acc is None else [acc]

    def place(i, idx):
        return (lax.div(idx[i], 2), 0, lax.rem(idx[i], 2), 0, 0)

    block = pl.BlockSpec((1, 2, 1, depth // 2, width), place)
    return pl.pallas_call(
        functools.partial(mix_kernel, n),
        grid_spec=pltpu.PrefetchScalarGridSpec(
            num_scalar_prefetch=1,
            grid=(n,),
            in_specs=[block] + [whole] * (2 * n + len(extra)),
            out_specs=pl.BlockSpec((2 * rows, width), lambda i, idx: (0, 0)),
        ),
        out_shape=jax.ShapeDtypeStruct((2 * rows, width), F32 if n > 1 else BF16),
        compiler_params=pltpu.CompilerParams(vmem_limit_bytes=40 * MIB),
        cost_estimate=pl.CostEstimate(
            flops=4 * rows * n * depth * width, bytes_accessed=n * 3 * MIB, transcendentals=0
        ),
    )(idx, wo, *first, *second, *extra)


def select(table, k):
    return sum(jnp.where(k == i, v, 0) for i, v in enumerate(table))


class Live(dict):

    def __getattr__(self, name):
        return self[name]

    def __setattr__(self, name, value):
        self[name] = value

    def sync(self):
        names = sorted(self)
        self.update(zip(names, lax.optimization_barrier([self[k] for k in names])))

    def drop(self, *names):
        for name in names:
            del self[name]


def on_device(hidden, wqkv, wo, picks):
    seqs, rows, feats = hidden.shape
    hidden = hidden.reshape(seqs * rows, feats)
    yh, x, core = lax.axis_index("yh"), lax.axis_index("x"), lax.axis_index("core")
    z, yl = lax.axis_index("z"), lax.axis_index("yl")
    lblocks = rows // BLOCK
    first = (yh * 4 + x) * 2 + core
    cosine, sine = tables(first, rows)
    qn = G * HD

    def blocks(c):
        back = jnp.where(c == 0, x + 3, x + 1) % 4
        out = []
        for a in range(2):
            for xx, cc in ((x, c), (back, c), (back, 1 - c), ((x + 2) % 4, c)):
                out.append(((yh ^ a) * 4 + xx) * 2 + cc)
        return jnp.stack(out).astype(jnp.int32)

    def slot_of(yy, xx, cc):
        turn = jnp.where(core == 0, xx - x, x - xx) % 4
        table = (0, 1, 11, 10, 4, 14, 2, 3, 5, 6, 13, 12, 9, 15, 7, 8)
        return select(table, (yy ^ yh) * 8 + turn * 2 + (cc ^ core))

    mine = lax.dynamic_slice_in_dim(picks, first * lblocks, lblocks, 1)
    owner, sub = mine // lblocks, mine % lblocks
    seq = jnp.arange(seqs)[:, None, None]
    idx = slot_of(owner // 8, (owner // 2) % 4, owner % 2) * (seqs * lblocks) + seq * lblocks + sub
    idx = idx.reshape(seqs * lblocks, KB).astype(jnp.int32)

    v = Live(w=wqkv, wo=wo)
    qh = HALF * HD
    v.w_n = step_x(v.w)
    v.w_c = swap(v.w, "core")
    v.kv_y = swap(v.w[:, qn:], "yh")
    v.q1_y = swap(v.w[:, :qh], "yh")
    v.sync()
    v.w_m = step_x(v.w_c)
    v.kv_yn = step_x(v.kv_y)
    v.kv_yc, v.q1_yc = swap(v.kv_y, "core"), swap(v.q1_y, "core")
    v.q0_y = swap(v.w[:, qh:qn], "yh")
    v.wo_a = swap(v.wo[:256], "yh")
    v.h_send = pick_columns(hidden, blocks(1 - core))
    v.h_own = pick_columns(hidden, blocks(core))
    v.sync()
    v.kv_ym, v.kv_yf = step_x(v.kv_yc), step_x(v.kv_yn)
    v.w_f = step_x(v.w_n)
    v.q0_yn = swap(v.w_n[:, qh:qn], "yh")
    v.h_part = swap(v.h_send, "core")
    v.drop("h_send")
    v.sync()

    def pieces_of(name, col):
        ends = ("_y", "_yn", "_ym", "_yf")
        return [(v.w, col), (v.w_n, col), (v.w_m, col), (v.w_f, col)] + [(v[name + e], 0) for e in ends]

    v.q1_yn, v.q1_ym = step_x(v.q1_y), step_x(v.q1_yc)
    v.q0_ym = swap(v.w_m[:, qh:qn], "yh")
    v.kv_part, v.kv_own = project(v.h_part, v.h_own, pieces_of("kv", qn), 2 * HD)
    v.wo_b = swap(v.wo[256:], "yh")
    v.sync()
    v.wo2 = rows_of(v.wo, v.wo_a, v.wo_b)
    v.drop("wo", "wo_a", "wo_b")
    v.kv_got = swap(v.kv_part, "core")
    v.sync()
    kv = v.kv_own + v.kv_got
    keys = kv[:, :HD].reshape(seqs, rows, HD)
    keys = keys * cosine + jnp.roll(keys, HD // 2, -1) * sine
    v.p = jnp.concatenate([keys.reshape(seqs * rows, HD), kv[:, HD:]], -1).astype(BF16)
    v.p_n = step_x(v.p)
    v.p_c = swap(v.p, "core")
    v.p_y = swap(v.p, "yh")
    v.q1_yf = step_x(v.q1_yn)
    v.sync()
    wo_all = lax.all_gather(v.wo2, ("x", "core"), axis=0, tiled=True).reshape(4, 2, 2, 512, wo.shape[1])
    v.drop("wo2")
    v.p_m, v.p_yn, v.p_f = step_x(v.p_c), step_x(v.p_y), step_x(v.p_n)
    v.p_yc = swap(v.p_y, "core")
    v.q0_yf = swap(v.w_f[:, qh:qn], "yh")
    v.q1_part, v.q1_own = project(v.h_part, v.h_own, pieces_of("q1", 0), qh)
    v.sync()
    v.p_ym, v.p_yf = step_x(v.p_yc), step_x(v.p_yn)
    v.p_nc, v.p_mc, v.p_ync, v.p_fc = [swap(v["p_" + k], "core") for k in ("n", "m", "yn", "f")]
    v.q0_part, v.q0_own = project(v.h_part, v.h_own, pieces_of("q0", qh), qh)
    v.sync()
    v.q0_got, v.q1_got = swap(v.q0_part, "core"), swap(v.q1_part, "core")
    v.p_ymc, v.p_yfc = swap(v.p_ym, "core"), swap(v.p_yf, "core")
    v.sync()
    ends = ("", "_c", "_n", "_m", "_f", "_y", "_yc", "_yn", "_ym", "_yf", "_nc", "_mc", "_ync", "_ymc", "_fc", "_yfc")
    pieces = [v["p" + e] for e in ends]
    queries = [v.q1_own, v.q1_got, v.q0_own, v.q0_got]
    def group(*at):
        blocks = [((z + d) % 4) * 2 + (yl ^ a) for a, d in at]
        return jnp.stack([(c % 4) * 2 + ((c // 4) ^ yh) for c in blocks]).astype(jnp.int32)

    v = Live(
        s0=attend(0, queries, cosine, sine, pieces, idx, lblocks),
        s1=attend(1, queries, cosine, sine, pieces, idx, lblocks),
    )
    v.a_y = swap(v.s0, "yl")
    v.a_l, v.a_r = shift_z(v.s0, 1), shift_z(v.s0, -1)
    v.b_l, v.b_r = shift_z(v.s1, 1), shift_z(v.s1, -1)
    v.b_y = swap(v.s1, "yl")
    v.sync()
    v.a_yl, v.a_yr = shift_z(v.a_y, 1), shift_z(v.a_y, -1)
    v.a_f = shift_z(v.a_l, 1)
    v.b_f = shift_z(v.b_r, -1)
    v.b_ly, v.b_ry = swap(v.b_l, "yl"), swap(v.b_r, "yl")
    v.t = mix([v.s0, v.a_l, v.a_r, v.a_y], [v.s1, v.b_l, v.b_r, v.b_y], wo_all, group((0, 0), (0, 3), (0, 1), (1, 0)))
    v.sync()
    v.a_yf = shift_z(v.a_yl, 1)
    v.b_fy = swap(v.b_f, "yl")

    late = group((1, 3), (1, 1), (0, 2))
    v.t = mix([v.a_yl, v.a_yr, v.a_f], [v.b_ly, v.b_ry, v.b_f], wo_all, late, v.t)
    v.sync()
    return mix([v.a_yf], [v.b_fy], wo_all, group((1, 2)), v.t).reshape(seqs, rows, wo.shape[1])


def solution(mesh):
    fine = Mesh(mesh.devices.reshape(2, 4, 2, 4, 2), ("yh", "x", "core", "z", "yl"))
    row, col = ("yh", "x", "core"), ("z", "yl")
    return jax.shard_map(
        on_device,
        mesh=fine,
        in_specs=(P(None, row, None), P(row, col), P(row, col), P()),
        out_specs=P(None, row, col),
        check_vma=False,
    )
```

```python
import functools
import math

import jax
import jax.numpy as jnp
from jax import lax
from jax.experimental import pallas as pl
from jax.experimental.pallas import tpu as pltpu
from jax.sharding import Mesh
from jax.sharding import PartitionSpec as P

HD = 128
BLOCK = 128
KB = 8
G = 8
HALF = G // 2
rope_base = 500000.0
F32 = jnp.float32
BF16 = jnp.bfloat16
MIB = 2**20


def swap(a, axis):
    return lax.ppermute(a, axis, [(0, 1), (1, 0)])


def step_x(a):
    pairs = []
    for x in range(4):
        pairs.append((2 * x, 2 * ((x + 1) % 4)))
        pairs.append((2 * x + 1, 2 * ((x - 1) % 4) + 1))
    return lax.ppermute(a, ("x", "core"), pairs)


def shift_z(a, step):
    return lax.ppermute(a, "z", [(i, (i + step) % 4) for i in range(4)])


def rows_of(*parts):
    return jnp.concatenate(parts, 0)


def tables(first, rows):
    half = HD // 2
    index = jnp.arange(half).astype(F32)
    inverse = jnp.exp(-math.log(rope_base) * 2.0 * index / HD)
    positions = first * rows + jnp.arange(rows)
    angle = positions.astype(F32)[:, None] * inverse[None, :]
    cosine, sine = jnp.cos(angle), jnp.sin(angle)
    return jnp.concatenate([cosine, cosine], -1), jnp.concatenate([-sine, sine], -1)


def pick_kernel(idx, in_ref, out_ref):
    out_ref[...] = in_ref[...]


def pick_columns(a, idx):
    rows, n = a.shape[0], idx.shape[0]
    return pl.pallas_call(
        pick_kernel,
        grid_spec=pltpu.PrefetchScalarGridSpec(
            num_scalar_prefetch=1,
            grid=(n,),
            in_specs=[pl.BlockSpec((rows, 512), lambda i, idx: (0, idx[i]))],
            out_specs=pl.BlockSpec((rows, 512), lambda i, idx: (0, i)),
        ),
        out_shape=jax.ShapeDtypeStruct((rows, n * 512), a.dtype),
        compiler_params=pltpu.CompilerParams(vmem_limit_bytes=16 * MIB),
        cost_estimate=pl.CostEstimate(flops=0, bytes_accessed=16 * MIB, transcendentals=0),
    )(idx, a)


def project_kernel(cols, part_h, own_h, *refs):
    n = len(cols)
    pieces, (part_ref, own_ref, h_ref, w_ref, sem) = refs[:n], refs[n:]
    rows, width = part_ref.shape
    copies = []
    for k in range(n):
        at = pl.ds(k * 512, 512)
        copies.append(
            (
                pltpu.make_async_copy(pieces[k].at[:, pl.ds(cols[k], width)], w_ref.at[at], sem.at[k, 0]),
                pltpu.make_async_copy(part_h.at[:, at], h_ref.at[pl.ds(0, rows), at], sem.at[k, 1]),
                pltpu.make_async_copy(own_h.at[:, at], h_ref.at[pl.ds(rows, rows), at], sem.at[k, 2]),
            )
        )
        for copy in copies[-1]:
            copy.start()
    for k in range(0, n, 2):
        for copy in copies[k] + copies[k + 1]:
            copy.wait()
        at = slice(k * 512, (k + 2) * 512)
        t = jnp.dot(h_ref[:, at], w_ref[at], preferred_element_type=F32)
        if k == 0:
            part_ref[...], own_ref[...] = t[:rows], t[rows:]
        else:
            part_ref[...] += t[:rows]
            own_ref[...] += t[rows:]


def project(h_part, h_own, pieces, width):
    n, rows = len(pieces), h_part.shape[0]
    away, whole = pl.BlockSpec(memory_space=pl.ANY), pl.BlockSpec(memory_space=pltpu.VMEM)
    return pl.pallas_call(
        functools.partial(project_kernel, tuple(col for _, col in pieces)),
        in_specs=[away] * (n + 2),
        out_specs=[whole] * 2,
        out_shape=[jax.ShapeDtypeStruct((rows, width), F32)] * 2,
        scratch_shapes=[
            pltpu.VMEM((2 * rows, n * 512), BF16),
            pltpu.VMEM((n * 512, width), BF16),
            pltpu.SemaphoreType.DMA((n, 3)),
        ],
        compiler_params=pltpu.CompilerParams(vmem_limit_bytes=60 * MIB),
        cost_estimate=pl.CostEstimate(
            flops=4 * rows * n * 512 * width, bytes_accessed=12 * MIB, transcendentals=0
        ),
    )(h_part, h_own, *[p for p, _ in pieces])


def attend_kernel(offset, idx, q1a_ref, q1b_ref, q0a_ref, q0b_ref, cos_ref, sin_ref, *refs):
    pieces, out_ref, kv_ref, sem = refs[:-3], refs[-3], refs[-2], refs[-1]
    n = pl.program_id(0)

    @pl.when(n == 0)
    def _():
        at, copies = 0, []
        for k, p in enumerate(pieces):
            copies.append(pltpu.make_async_copy(p, kv_ref.at[pl.ds(at, p.shape[0])], sem.at[k]))
            copies[-1].start()
            at += p.shape[0]
        for copy in copies:
            copy.wait()

    cosine, sine = cos_ref[...], sin_ref[...]
    heads = []
    for g in range(G):
        cols = slice(g % HALF * HD, (g % HALF + 1) * HD)
        one, two = (q1a_ref, q1b_ref) if g < HALF else (q0a_ref, q0b_ref)
        t = one[:, cols] + two[:, cols]
        heads.append((t * cosine + pltpu.roll(t, HD // 2, 1) * sine).astype(BF16))
    q = jnp.concatenate(heads, 0)
    places = [pl.multiple_of(idx[offset + n, j] * BLOCK, BLOCK) for j in range(KB)]
    keys = jnp.concatenate([kv_ref[pl.ds(p, BLOCK), :HD] for p in places], 0)
    values = jnp.concatenate([kv_ref[pl.ds(p, BLOCK), HD:] for p in places], 0)
    s = lax.dot_general(q, keys, (((1,), (1,)), ((), ())), preferred_element_type=F32)
    top = jnp.max(s, -1, keepdims=True)
    e = jnp.exp2((s - top) * (math.log2(math.e) / math.sqrt(HD)))
    total = jnp.sum(e, -1, keepdims=True)
    o = jnp.dot(e.astype(BF16), values, preferred_element_type=F32) / total
    o = o.astype(BF16)
    for g in range(G):
        out_ref[:, g * HD : (g + 1) * HD] = o[g * BLOCK : (g + 1) * BLOCK]


def attend(seq, queries, cosine, sine, pieces, idx, lblocks):
    first = seq * lblocks
    rows = sum(p.shape[0] for p in pieces)
    away = pl.BlockSpec(memory_space=pl.ANY)
    return pl.pallas_call(
        functools.partial(attend_kernel, first),
        grid_spec=pltpu.PrefetchScalarGridSpec(
            num_scalar_prefetch=1,
            grid=(lblocks,),
            in_specs=[
                pl.BlockSpec((BLOCK, HALF * HD), lambda n, idx: (first + n, 0)),
            ]
            * 4
            + [pl.BlockSpec((BLOCK, HD), lambda n, idx: (n, 0))] * 2
            + [away] * len(pieces),
            out_specs=pl.BlockSpec((BLOCK, G * HD), lambda n, idx: (n, 0)),
            scratch_shapes=[pltpu.VMEM((rows, 2 * HD), BF16), pltpu.SemaphoreType.DMA((len(pieces),))],
        ),
        out_shape=jax.ShapeDtypeStruct((lblocks * BLOCK, G * HD), BF16),
        compiler_params=pltpu.CompilerParams(vmem_limit_bytes=60 * MIB),
        cost_estimate=pl.CostEstimate(flops=10**9, bytes_accessed=6 * MIB, transcendentals=2 * MIB),
    )(idx, *queries, cosine, sine, *pieces)


def mix_kernel(count, idx, w_ref, *refs):
    acc_ref, out_ref = refs[-2:] if len(refs) == 2 * count + 2 else (None, refs[-1])
    i = pl.program_id(0)
    half = refs[0].shape[0]

    if count > 1:

        @pl.when(i == 0)
        def _():
            out_ref[...] = jnp.zeros_like(out_ref) if acc_ref is None else acc_ref[...]

        for k in range(count):

            @pl.when(i == k)
            def _(k=k):
                a = jnp.concatenate([refs[k][...], refs[count + k][...]], 0)
                out_ref[...] += jnp.dot(a, w_ref[...], preferred_element_type=F32)

    else:
        for k in range(2):
            rows = slice(k * half, (k + 1) * half)
            t = acc_ref[rows] + jnp.dot(refs[k][...], w_ref[...], preferred_element_type=F32)
            out_ref[rows] = t.astype(out_ref.dtype)


def mix(first, second, wo, idx, acc=None):
    rows, depth = first[0].shape
    n, width = len(first), wo.shape[1]
    whole = pl.BlockSpec(memory_space=pltpu.VMEM)
    extra = [] if acc is None else [acc]
    return pl.pallas_call(
        functools.partial(mix_kernel, n),
        grid_spec=pltpu.PrefetchScalarGridSpec(
            num_scalar_prefetch=1,
            grid=(n,),
            in_specs=[pl.BlockSpec((depth, width), lambda i, idx: (idx[i], 0))] + [whole] * (2 * n + len(extra)),
            out_specs=pl.BlockSpec((2 * rows, width), lambda i, idx: (0, 0)),
        ),
        out_shape=jax.ShapeDtypeStruct((2 * rows, width), F32 if n > 1 else BF16),
        compiler_params=pltpu.CompilerParams(vmem_limit_bytes=40 * MIB),
        cost_estimate=pl.CostEstimate(
            flops=4 * rows * n * depth * width, bytes_accessed=n * 3 * MIB, transcendentals=0
        ),
    )(idx, wo, *first, *second, *extra)


def select(table, k):
    return sum(jnp.where(k == i, v, 0) for i, v in enumerate(table))


class Live(dict):

    def __getattr__(self, name):
        return self[name]

    def __setattr__(self, name, value):
        self[name] = value

    def sync(self):
        names = sorted(self)
        self.update(zip(names, lax.optimization_barrier([self[k] for k in names])))

    def drop(self, *names):
        for name in names:
            del self[name]


def on_device(hidden, wqkv, wo, picks):
    seqs, rows, feats = hidden.shape
    hidden = hidden.reshape(seqs * rows, feats)
    yh, x, core = lax.axis_index("yh"), lax.axis_index("x"), lax.axis_index("core")
    z, yl = lax.axis_index("z"), lax.axis_index("yl")
    lblocks = rows // BLOCK
    first = (yh * 4 + x) * 2 + core
    cosine, sine = tables(first, rows)
    qn = G * HD

    def blocks(c):
        back = jnp.where(c == 0, x + 3, x + 1) % 4
        out = []
        for a in range(2):
            for xx, cc in ((x, c), (back, c), (back, 1 - c), ((x + 2) % 4, c)):
                out.append(((yh ^ a) * 4 + xx) * 2 + cc)
        return jnp.stack(out).astype(jnp.int32)

    def slot_of(yy, xx, cc):
        turn = jnp.where(core == 0, xx - x, x - xx) % 4
        table = (0, 1, 11, 10, 4, 14, 2, 3, 5, 6, 13, 12, 9, 15, 7, 8)
        return select(table, (yy ^ yh) * 8 + turn * 2 + (cc ^ core))

    mine = lax.dynamic_slice_in_dim(picks, first * lblocks, lblocks, 1)
    owner, sub = mine // lblocks, mine % lblocks
    seq = jnp.arange(seqs)[:, None, None]
    idx = slot_of(owner // 8, (owner // 2) % 4, owner % 2) * (seqs * lblocks) + seq * lblocks + sub
    idx = idx.reshape(seqs * lblocks, KB).astype(jnp.int32)

    v = Live(w=wqkv, wo=wo)
    qh = HALF * HD
    v.w_n = step_x(v.w)
    v.w_c = swap(v.w, "core")
    v.kv_y = swap(v.w[:, qn:], "yh")
    v.q1_y = swap(v.w[:, :qh], "yh")
    v.sync()
    v.w_m = step_x(v.w_c)
    v.kv_yn = step_x(v.kv_y)
    v.kv_yc, v.q1_yc = swap(v.kv_y, "core"), swap(v.q1_y, "core")
    v.q0_y = swap(v.w[:, qh:qn], "yh")
    v.h_send = pick_columns(hidden, blocks(1 - core))
    v.h_own = pick_columns(hidden, blocks(core))
    v.sync()
    v.kv_ym, v.kv_yf = step_x(v.kv_yc), step_x(v.kv_yn)
    v.w_f = step_x(v.w_n)
    v.q0_yn = swap(v.w_n[:, qh:qn], "yh")
    v.h_part = swap(v.h_send, "core")
    v.drop("h_send")
    v.sync()

    def pieces_of(name, col):
        ends = ("_y", "_yn", "_ym", "_yf")
        return [(v.w, col), (v.w_n, col), (v.w_m, col), (v.w_f, col)] + [(v[name + e], 0) for e in ends]

    v.q1_yn, v.q1_ym = step_x(v.q1_y), step_x(v.q1_yc)
    v.q0_ym = swap(v.w_m[:, qh:qn], "yh")
    v.kv_part, v.kv_own = project(v.h_part, v.h_own, pieces_of("kv", qn), 2 * HD)
    v.sync()
    wo_all = lax.all_gather(v.wo, ("yh", "x", "core"), axis=0, tiled=True)
    v.drop("wo")
    v.kv_got = swap(v.kv_part, "core")
    v.sync()
    kv = v.kv_own + v.kv_got
    keys = kv[:, :HD].reshape(seqs, rows, HD)
    keys = keys * cosine + jnp.roll(keys, HD // 2, -1) * sine
    v.p = jnp.concatenate([keys.reshape(seqs * rows, HD), kv[:, HD:]], -1).astype(BF16)
    v.p_n = step_x(v.p)
    v.p_c = swap(v.p, "core")
    v.p_y = swap(v.p, "yh")
    v.q1_yf = step_x(v.q1_yn)
    v.sync()
    v.p_m, v.p_yn, v.p_f = step_x(v.p_c), step_x(v.p_y), step_x(v.p_n)
    v.p_yc = swap(v.p_y, "core")
    v.q0_yf = swap(v.w_f[:, qh:qn], "yh")
    v.q1_part, v.q1_own = project(v.h_part, v.h_own, pieces_of("q1", 0), qh)
    v.sync()
    v.p_ym, v.p_yf = step_x(v.p_yc), step_x(v.p_yn)
    v.p_nc, v.p_mc, v.p_ync, v.p_fc = [swap(v["p_" + k], "core") for k in ("n", "m", "yn", "f")]
    v.q0_part, v.q0_own = project(v.h_part, v.h_own, pieces_of("q0", qh), qh)
    v.sync()
    v.q0_got, v.q1_got = swap(v.q0_part, "core"), swap(v.q1_part, "core")
    v.p_ymc, v.p_yfc = swap(v.p_ym, "core"), swap(v.p_yf, "core")
    v.sync()
    ends = ("", "_c", "_n", "_m", "_f", "_y", "_yc", "_yn", "_ym", "_yf", "_nc", "_mc", "_ync", "_ymc", "_fc", "_yfc")
    pieces = [v["p" + e] for e in ends]
    queries = [v.q1_own, v.q1_got, v.q0_own, v.q0_got]
    def group(*at):
        return jnp.stack([((z + d) % 4) * 2 + (yl ^ a) for a, d in at]).astype(jnp.int32)

    v = Live(
        s0=attend(0, queries, cosine, sine, pieces, idx, lblocks),
        s1=attend(1, queries, cosine, sine, pieces, idx, lblocks),
    )
    v.a_y = swap(v.s0, "yl")
    v.a_l, v.a_r = shift_z(v.s0, 1), shift_z(v.s0, -1)
    v.b_l, v.b_r = shift_z(v.s1, 1), shift_z(v.s1, -1)
    v.b_y = swap(v.s1, "yl")
    v.sync()
    v.a_yl, v.a_yr = shift_z(v.a_y, 1), shift_z(v.a_y, -1)
    v.a_f = shift_z(v.a_l, 1)
    v.b_f = shift_z(v.b_r, -1)
    v.b_ly, v.b_ry = swap(v.b_l, "yl"), swap(v.b_r, "yl")
    v.t = mix([v.s0, v.a_l, v.a_r, v.a_y], [v.s1, v.b_l, v.b_r, v.b_y], wo_all, group((0, 0), (0, 3), (0, 1), (1, 0)))
    v.sync()
    v.a_yf = shift_z(v.a_yl, 1)
    v.b_fy = swap(v.b_f, "yl")

    late = group((1, 3), (1, 1), (0, 2))
    v.t = mix([v.a_yl, v.a_yr, v.a_f], [v.b_ly, v.b_ry, v.b_f], wo_all, late, v.t)
    v.sync()
    return mix([v.a_yf], [v.b_fy], wo_all, group((1, 2)), v.t).reshape(seqs, rows, wo.shape[1])


def solution(mesh):
    fine = Mesh(mesh.devices.reshape(2, 4, 2, 4, 2), ("yh", "x", "core", "z", "yl"))
    row, col = ("yh", "x", "core"), ("z", "yl")
    return jax.shard_map(
        on_device,
        mesh=fine,
        in_specs=(P(None, row, None), P(row, col), P(row, col), P()),
        out_specs=P(None, row, col),
        check_vma=False,
    )
```
